512 devices in a mesh: occ: 32 (over z_hi, x, core), virt: 16 (over z_lo, y).
Axes of the slice: x: 4, y: 8, z: 8 (z_hi: 4, z_lo: 2; z = z_hi * 2 + z_lo), core: 2. Of those that a mesh axis runs over, the one named last changes fastest.
Arguments:
- amplitudes: bfloat16 [8192, 4096], P('occ', 'virt'), may hold values from -6 to 6
- screen: int32 [64, 32], P('occ', 'virt'), may hold values 0 or 1
- hole_ints: bfloat16 [8192, 8192], P('occ'), may hold values from -0.09375 to 0.09375
- particle_ints: bfloat16 [4096, 4096], P('virt', 'occ'), may hold values from -0.125 to 0.125
- direct_ints: bfloat16 [8192, 4096], P('occ', 'virt'), may hold values from -6 to 6
- occ_energy: float32 [8192], P('occ'), may hold values from -3 to -0.5
- virt_energy: float32 [4096], P('virt'), may hold values from 0.5 to 4
Outputs:
- residual: float32 [8192, 4096], P('occ', 'virt')
- updated: bfloat16 [8192, 4096], P('occ', 'virt')
The draws below stay inside these ranges and needn't reach their ends.
All inputs are finite; a program needn't handle non-finite values. No bound on the sum of `screen` on one device may be relied on, other than what follows from the above.
Results may differ from the reference program's by a relative error of at most 0.001.
Values may be sent and summed in bfloat16 or wider, within the bound.
A program may use at most 64 MiB of HBM per device.

```python
import jax
import jax.numpy as jnp

TILE = 128
NOB = 64
NVB = 32
NO = 8192
NV = 4096


def plant(result, rng, least, largest):
    extent = result.shape
    index_at = [jax.random.randint(jax.random.fold_in(rng, axis), (), 0, extent[axis]) for axis in range(len(extent))]
    result = result.at[tuple(index_at)].set(least)
    longest = extent.index(max(extent))
    index_at[longest] = (index_at[longest] + 1) % extent[longest]
    return result.at[tuple(index_at)].set(largest)


def levels(key, shape, shards, low, largest):
    loudness = 1.0
    for position, blocks in shards:
        heights = jax.random.uniform(jax.random.fold_in(jax.random.fold_in(key, 6), position), (blocks,), jnp.float32, low / len(shards), largest / len(shards))
        loudness = loudness * jnp.repeat(jnp.exp(heights), shape[position] // blocks).reshape((-1,) + (1,) * (len(shape) - 1 - position))
    return loudness


def normal_values(key, shape, deviation, bound, cuts=(), kind=jnp.bfloat16):
    result = jax.random.normal(key, shape, jnp.float32) * deviation
    if len(cuts) > 0:
        result = levels(key, shape, cuts, -0.22, 0.18) * result
    return jnp.clip(result, min=-bound, max=bound).astype(kind)


def setup_inputs(seed: int = 0) -> dict:
    key_list = jax.random.split(jax.random.key(seed), 8)
    return {
        "amplitudes": normal_values(key_list[0], (NO, NV), 1.0, 6.0, ((0, 32), (1, 16))),
        "screen": plant((jax.random.randint(key_list[1], (NOB, NVB), 0, 2) < 1).astype(jnp.int32), jax.random.fold_in(key_list[1], 1), 0, 1),
        "hole_ints": normal_values(key_list[2], (NO, NO), (NO // 2) ** -0.5, 0.09375, ((0, 32),)),
        "particle_ints": normal_values(key_list[3], (NV, NV), (NV // 2) ** -0.5, 0.125, ((0, 16), (1, 32))),
        "direct_ints": normal_values(key_list[4], (NO, NV), 1.0, 6.0, ((0, 32), (1, 16))),
        "occ_energy": jnp.clip(-3.0 + 2.5 * jax.random.uniform(key_list[5], (NO,), jnp.float32) ** levels(key_list[5], (NO,), ((0, 32),), -0.2, 0.2), -3.0, -0.5),
        "virt_energy": jnp.clip(0.5 + 3.5 * jax.random.uniform(key_list[6], (NV,), jnp.float32) ** levels(key_list[6], (NV,), ((0, 16),), -0.2, 0.2), 0.5, 4.0),
    }


def reference(amplitudes, screen, hole_ints, particle_ints, direct_ints, occ_energy, virt_energy):
    keep = jnp.repeat(jnp.repeat(screen, TILE, 0), TILE, 1).astype(jnp.float32)
    screened = (amplitudes.astype(jnp.float32) * keep).astype(jnp.bfloat16)
    hole = jnp.dot(hole_ints, screened, preferred_element_type=jnp.float32)
    particle = jnp.dot(screened, particle_ints, preferred_element_type=jnp.float32)
    denom = virt_energy[None, :] - occ_energy[:, None]
    amps = amplitudes.astype(jnp.float32)
    residual = keep * (direct_ints.astype(jnp.float32) + hole + particle - denom * amps)
    updated = (amps + residual / denom).astype(jnp.bfloat16)
    return residual, updated
```

```python
import functools

import jax
import jax.numpy as jnp
from jax import lax
from jax.experimental import pallas as pl
from jax.experimental.pallas import tpu as pltpu
from jax.sharding import PartitionSpec as P

MESH = pl.DeviceIdType.MESH
NX, NZH, NY, NZL = 4, 4, 8, 2
ROWS, COLS, HALF, TILE = 256, 256, 128, 128


def wrap(a, n):
    return lax.rem(a + n, n)


class Links:
    def __init__(self, send_sem, recv_sem):
        self.send_sem, self.recv_sem = send_sem, recv_sem
        self.ids, self.sent = {}, []

    def _copy(self, name, src, dst, device):
        n = self.ids.setdefault(name, len(self.ids))
        return pltpu.make_async_remote_copy(
            src_ref=src,
            dst_ref=dst,
            send_sem=self.send_sem.at[n],
            recv_sem=self.recv_sem.at[n],
            device_id=device,
            device_id_type=MESH,
        )

    def send(self, name, src, device, dst=None):
        copy = self._copy(name, src, src if dst is None else dst, device)
        copy.start()
        self.sent.append(copy)

    def recv(self, name, dst, device):
        self._copy(name, dst, dst, device).wait_recv()

    def drain(self):
        for copy in self.sent:
            copy.wait_send()


N_COPIES = 96


def kernel(
    screen_ref,
    amps_hbm,
    hole_hbm,
    part_hbm,
    direct_hbm,
    occ_ref,
    virt_ref,
    residual_ref,
    updated_ref,
    amps,
    direct,
    hole_ints,
    col,
    row,
    slab,
    total,
    send_sem,
    recv_sem,
    load_sem,
):
    o, v = lax.axis_index("occ"), lax.axis_index("virt")
    core, chip = lax.rem(o, 2), o // 2
    x, zh = lax.rem(chip, NX), chip // NX
    zl, y = v // NY, lax.rem(v, NY)

    def occ_of(zh, x, core):
        return (zh * NX + x) * 2 + core

    def zx(dz, dx):
        return wrap(zh + dz, NZH), wrap(x + dx, NX)

    def at_zx(dz, dx):
        return (occ_of(*zx(dz, dx), core), v)

    def at_y(dy):
        return (o, zl * NY + wrap(y + dy, NY))

    sibling = (occ_of(zh, x, 1 - core), v)
    partner = (o, (1 - zl) * NY + y)
    across = (v * 2 + core, chip)
    moves = chip != v

    load_amps = pltpu.make_async_copy(amps_hbm, amps, load_sem.at[0])
    load_amps.start()
    load_hole = pltpu.make_async_copy(hole_hbm, hole_ints, load_sem.at[1])
    load_direct = pltpu.make_async_copy(direct_hbm, direct, load_sem.at[2])
    load_hole.start()
    load_direct.start()

    barrier = pltpu.get_barrier_semaphore()
    near = [at_zx(1, 0), at_zx(-1, 0), at_zx(0, 1), at_zx(0, -1), at_y(1), at_y(-1), sibling, partner]
    for device in near:
        pl.semaphore_signal(barrier, inc=1, device_id=device, device_id_type=MESH)

    @pl.when(moves)
    def _():
        pl.semaphore_signal(barrier, inc=1, device_id=across, device_id_type=MESH)

    load_amps.wait()
    for i in range(2):
        for j in range(2):
            rows, cols = pl.ds(i * TILE, TILE), pl.ds(j * TILE, TILE)
            keep = screen_ref[i, j].astype(jnp.float32)
            tile = (amps[rows, cols].astype(jnp.float32) * keep).astype(jnp.bfloat16)
            col[o, rows, cols] = tile
            row[v, rows, cols] = tile

    pl.semaphore_wait(barrier, len(near) + moves.astype(jnp.int32))

    links = Links(send_sem, recv_sem)
    home = slab.at[core, chip]

    @pl.when(moves)
    def _():
        links._copy("across", part_hbm, slab.at[core, v], across).start()

    @pl.when(jnp.logical_not(moves))
    def _():
        pltpu.make_async_copy(part_hbm, home, load_sem.at[3]).start()

    class Gather:
        def __init__(self, tag, block):
            self.tag, self.block = tag, block

        def full(self, dz, dx):
            return self.block(*zx(dz, dx), core)

        def half(self, dz, dx, h):
            return self.full(dz, dx).at[pl.ds(h * HALF, HALF)]

        def name(self, *parts):
            return (self.tag,) + parts

        def z0(self):
            links.send(self.name("zf"), self.full(0, 0), at_zx(1, 0))
            links.send(self.name("zb"), self.full(0, 0), at_zx(-1, 0))

        def z1(self, way):
            tag = "f" if way == 1 else "b"
            h = 0 if way == 1 else 1
            links.recv(self.name("z" + tag), self.full(-way, 0), at_zx(-way, 0))
            links.send(self.name("zh" + tag), self.half(-way, 0, h), at_zx(way, 0))

        def z2(self):
            links.recv(self.name("zhf"), self.half(2, 0, 0), at_zx(-1, 0))
            links.recv(self.name("zhb"), self.half(2, 0, 1), at_zx(1, 0))

        def x0(self, dz):
            links.send(self.name("xf", dz), self.full(dz, 0), at_zx(0, 1))
            links.send(self.name("xb", dz), self.full(dz, 0), at_zx(0, -1))
            self.sib(dz, 0)

        def x1(self, dz):
            for way, tag, h in ((1, "f", 0), (-1, "b", 1)):
                links.recv(self.name("x" + tag, dz), self.full(dz, -way), at_zx(0, -way))
                links.send(self.name("xh" + tag, dz), self.half(dz, -way, h), at_zx(0, way))
            self.sib(dz, -1)
            self.sib(dz, 1)

        def x2(self, dz):
            links.recv(self.name("xhf", dz), self.half(dz, 2, 0), at_zx(0, -1))
            links.recv(self.name("xhb", dz), self.half(dz, 2, 1), at_zx(0, 1))
            self.sib(dz, 2)

        def sib(self, dz, dx):
            links.send(self.name("s", dz, dx), self.full(dz, dx), sibling)

        def from_sib(self, dz, dx):
            links.recv(self.name("s", dz, dx), self.block(*zx(dz, dx), 1 - core), sibling)

    amp = Gather("T", lambda zh, x, c: col.at[occ_of(zh, x, c)])
    ints = Gather("P", lambda zh, x, c: slab.at[c, zh * NX + x])

    def strip(e, dy):
        return row.at[(zl if e == 0 else 1 - zl) * NY + wrap(y + dy, NY)]

    def strip_half(e, dy, h):
        return strip(e, dy).at[pl.ds(h * HALF, HALF)]

    def y_send(e, hop):
        links.send(("y", e, hop, "f"), strip(e, 1 - hop), at_y(1))
        links.send(("y", e, hop, "b"), strip(e, hop - 1), at_y(-1))

    def y_recv(e, hop):
        links.recv(("y", e, hop, "f"), strip(e, -hop), at_y(-1))
        links.recv(("y", e, hop, "b"), strip(e, hop), at_y(1))

    def y_send_last(e):
        links.send(("y", e, 4, "f"), strip_half(e, -3, 0), at_y(1))
        links.send(("y", e, 4, "b"), strip_half(e, 3, 1), at_y(-1))

    def y_recv_last(e):
        links.recv(("y", e, 4, "f"), strip_half(e, 4, 0), at_y(-1))
        links.recv(("y", e, 4, "b"), strip_half(e, 4, 1), at_y(1))

    def add_hole(dz, dx):
        amp.from_sib(dz, dx)
        zz, xx = zx(dz, dx)
        c = zz * NX + xx
        block = col[pl.ds(c * 2, 2)].reshape(2 * ROWS, COLS)
        ints_ = hole_ints[:, pl.ds(pl.multiple_of(c * 512, 512), 512)]
        total[...] += jnp.dot(ints_, block, preferred_element_type=jnp.float32)

    amp.x0(0)
    amp.z0()
    y_send(0, 1)
    links.send(("pair",), row.at[v], partner)
    total[...] = jnp.zeros_like(total)
    amp.x1(0)
    y_recv(0, 1)
    y_send(0, 2)
    links.recv(("pair",), row.at[(1 - zl) * NY + y], partner)
    y_send(1, 1)
    amp.z1(1)
    amp.x0(-1)
    amp.z1(-1)
    amp.x0(1)

    @pl.when(moves)
    def _():
        links.recv("across", home, across)

    @pl.when(jnp.logical_not(moves))
    def _():
        pltpu.make_async_copy(part_hbm, home, load_sem.at[3]).wait()

    ints.z0()
    ints.x0(0)
    y_recv(1, 1)
    y_send(1, 2)
    y_recv(0, 2)
    y_send(0, 3)
    amp.x1(-1)
    amp.z2()
    amp.x0(2)
    load_hole.wait()
    add_hole(0, 0)
    y_recv(1, 2)
    y_send(1, 3)
    amp.x1(1)
    ints.x1(0)
    ints.z1(1)
    ints.x0(-1)
    ints.z1(-1)
    ints.x0(1)
    amp.x2(0)
    y_recv(0, 3)
    y_send_last(0)
    add_hole(0, 1)
    add_hole(0, -1)
    add_hole(-1, 0)
    add_hole(1, 0)
    amp.x1(2)
    ints.z2()
    ints.x0(2)
    y_recv(1, 3)
    y_send_last(1)
    amp.x2(-1)
    amp.x2(1)
    add_hole(-1, -1)
    add_hole(-1, 1)
    add_hole(0, 2)
    add_hole(2, 0)
    ints.x1(-1)
    ints.x1(1)
    add_hole(1, -1)
    add_hole(1, 1)
    add_hole(2, -1)
    add_hole(2, 1)
    ints.x2(0)
    amp.x2(2)
    ints.x1(2)
    ints.x2(-1)
    ints.x2(1)
    ints.x2(2)
    y_recv_last(0)
    y_recv_last(1)
    add_hole(-1, 2)
    add_hole(1, 2)
    add_hole(2, 2)
    for dz in (0, -1, 1, 2):
        for dx in (0, -1, 1, 2):
            ints.from_sib(dz, dx)

    for c in range(2):
        cols = pl.ds(c * TILE, TILE)

        def body(k, acc, c=c):
            return acc + jnp.dot(row[k], slab[c, k], preferred_element_type=jnp.float32)

        total[:, cols] = lax.fori_loop(0, 16, body, total[:, cols])

    load_direct.wait()
    occ_col = jnp.transpose(jnp.broadcast_to(occ_ref[...], (TILE, ROWS)))
    for i in range(2):
        for j in range(2):
            rows, cols = pl.ds(i * TILE, TILE), pl.ds(j * TILE, TILE)
            keep = screen_ref[i, j].astype(jnp.float32)
            a = amps[rows, cols].astype(jnp.float32)
            denom = virt_ref[:, cols] - occ_col[i * TILE : (i + 1) * TILE]
            res = keep * (direct[rows, cols].astype(jnp.float32) + total[rows, cols] - denom * a)
            residual_ref[rows, cols] = res
            updated_ref[rows, cols] = (a + res / denom).astype(jnp.bfloat16)

    @pl.when(moves)
    def _():
        links._copy("across", part_hbm, home, across).wait_send()

    links.drain()
    assert len(links.ids) <= N_COPIES


def on_device(amplitudes, screen, hole_ints, particle_ints, direct_ints, occ_energy, virt_energy):
    vmem, hbm = pl.BlockSpec(memory_space=pltpu.VMEM), pl.BlockSpec(memory_space=pl.ANY)
    return pl.pallas_call(
        kernel,
        out_shape=(
            jax.ShapeDtypeStruct((ROWS, COLS), jnp.float32),
            jax.ShapeDtypeStruct((ROWS, COLS), jnp.bfloat16),
        ),
        in_specs=[pl.BlockSpec(memory_space=pltpu.SMEM), hbm, hbm, hbm, hbm, vmem, vmem],
        out_specs=(vmem, vmem),
        scratch_shapes=[
            pltpu.VMEM((ROWS, COLS), jnp.bfloat16),
            pltpu.VMEM((ROWS, COLS), jnp.bfloat16),
            pltpu.VMEM((ROWS, 8192), jnp.bfloat16),
            pltpu.VMEM((32, ROWS, COLS), jnp.bfloat16),
            pltpu.VMEM((16, ROWS, COLS), jnp.bfloat16),
            pltpu.VMEM((2, 16, ROWS, TILE), jnp.bfloat16),
            pltpu.VMEM((ROWS, COLS), jnp.float32),
            pltpu.SemaphoreType.DMA((N_COPIES,)),
            pltpu.SemaphoreType.DMA((N_COPIES,)),
            pltpu.SemaphoreType.DMA((4,)),
        ],
        compiler_params=pltpu.CompilerParams(
            collective_id=0, has_side_effects=True, vmem_limit_bytes=40 * 2**20
        ),
        name="ladders",
    )(
        screen,
        amplitudes,
        hole_ints,
        particle_ints,
        direct_ints,
        occ_energy.reshape(1, ROWS),
        virt_energy.reshape(1, COLS),
    )


def solution(mesh):
    in_specs = (
        P("occ", "virt"),
        P("occ", "virt"),
        P("occ", None),
        P("virt", "occ"),
        P("occ", "virt"),
        P("occ"),
        P("virt"),
    )
    out_specs = (P("occ", "virt"), P("occ", "virt"))
    return jax.shard_map(
        on_device, mesh=mesh, in_specs=in_specs, out_specs=out_specs, check_vma=False
    )
```

```python
import functools

import jax
import jax.numpy as jnp
from jax import lax
from jax.experimental import pallas as pl
from jax.experimental.pallas import tpu as pltpu
from jax.sharding import PartitionSpec as P

MESH = pl.DeviceIdType.MESH
NX, NZH, NY, NZL = 4, 4, 8, 2
ROWS, COLS, HALF, TILE = 256, 256, 128, 128


def wrap(a, n):
    return lax.rem(a + n, n)


class Links:
    KINDS = "Typ12"

    def __init__(self, send_sem, recv_sem):
        self.send_sem, self.recv_sem = send_sem, recv_sem
        self.ids, self.sent = {}, {}

    def copy(self, name, src, dst, device):
        n = self.ids.setdefault(name, len(self.ids))
        return pltpu.make_async_remote_copy(
            src_ref=src,
            dst_ref=dst,
            send_sem=self.send_sem.at[self.KINDS.index(name[0][0])],
            recv_sem=self.recv_sem.at[n],
            device_id=device,
            device_id_type=MESH,
        )

    def send(self, name, src, device):
        self.copy(name, src, src, device).start()
        self.sent[name] = src.shape[0] * src.shape[1]

    def recv(self, name, dst, device):
        self.copy(name, dst, dst, device).wait_recv()

    def drain(self, kind, everything, device):
        sent = sum(size for name, size in self.sent.items() if name[0][0] == kind)
        assert sent == everything.shape[0] * everything.shape[1] * everything.shape[2]
        self.copy((kind,), everything, everything, device).wait_send()


N_COPIES = 112


def kernel(
    screen_hbm,
    amps_hbm,
    hole_hbm,
    part_hbm,
    direct_hbm,
    occ_hbm,
    virt_hbm,
    residual_ref,
    updated_ref,
    amps,
    direct,
    hole_ints,
    col,
    row,
    slab,
    moved,
    total,
    occ_ref,
    virt_ref,
    screen,
    send_sem,
    recv_sem,
    load_sem,
    z_sem,
):
    o, v = lax.axis_index("occ"), lax.axis_index("virt")
    core, chip = lax.rem(o, 2), o // 2
    x, zh = lax.rem(chip, NX), chip // NX
    zl, y = v // NY, lax.rem(v, NY)
    yl, y2 = lax.rem(y, 4), y // 4

    def occ_of(zh, x, core):
        return (zh * NX + x) * 2 + core

    def zx(dz, dx):
        return wrap(zh + dz, NZH), wrap(x + dx, NX)

    def at_zx(dz, dx):
        return (occ_of(*zx(dz, dx), core), v)

    def at_y(dy):
        return (o, zl * NY + wrap(y + dy, NY))

    def flipped(zh, hi, lo):
        return lax.rem(zh // 2 + hi, 2) * 2 + lax.rem(zh + lo, 2)

    sibling = (occ_of(zh, x, 1 - core), v)
    partner = (o, (1 - zl) * NY + y)
    zh_1 = flipped(zh, zl, y2)
    first_to = (occ_of(zh_1, wrap(x + yl, NX), core), v)
    first_from = (occ_of(zh_1, wrap(x - yl, NX), core), v)
    first_moves = v != 0
    v_2 = lax.rem(zh // 2 + zl, 2) * NY + lax.rem(zh + y2, 2) * 4 + wrap(x - yl, 4)
    second = (o, v_2)
    second_moves = v_2 != v

    def signal(sem, device):
        pl.semaphore_signal(sem, inc=1, device_id=device, device_id_type=MESH)

    first_plane = v + zh * 16 < NY
    later_plane = jnp.logical_not(first_plane)
    from_first = (zl == 0) & (zh == 1) & (y2 == 1)
    to_later = first_plane & (y2 == 1)
    barrier = pltpu.get_barrier_semaphore()
    plane = [at_zx(0, 1), at_zx(0, -1), at_y(1), at_y(-1), sibling]
    across = [
        (at_zx(1, 0), (zl == 0) & (zh == NZH - 1)),
        (at_zx(-1, 0), (zl == 0) & (zh == 1)),
        (partner, (zl == 1) & (zh == 0)),
    ]
    pl.when(first_moves & jnp.logical_not(from_first))(lambda: signal(barrier, first_from))
    pl.when(to_later)(lambda: signal(barrier, first_to))
    pl.when(second_moves)(lambda: signal(barrier, second))
    for device, to_first in across:
        pl.when(jnp.logical_not(to_first))(lambda device=device: signal(barrier, device))
    for device in plane:
        signal(barrier, device)

    loads = [
        pltpu.make_async_copy(src, dst, load_sem.at[n])
        for n, (src, dst) in enumerate(
            (
                (amps_hbm, amps),
                (hole_hbm, hole_ints),
                (direct_hbm, direct),
                (occ_hbm, occ_ref),
                (virt_hbm, virt_ref),
                (screen_hbm, screen),
            )
        )
    ]
    for load in loads:
        load.start()
    loads[0].wait()
    loads[5].wait()
    for i in range(2):
        for j in range(2):
            rows, cols = pl.ds(i * TILE, TILE), pl.ds(j * TILE, TILE)
            keep = screen[i : i + 1, j : j + 1].astype(jnp.float32)
            tile = (amps[rows, cols].astype(jnp.float32) * keep).astype(jnp.bfloat16)
            col[o, rows, cols] = tile
            row[v, rows, cols] = tile

    def count(*flags):
        return sum(flag.astype(jnp.int32) for flag in flags)

    pl.semaphore_wait(
        barrier,
        len(plane)
        + len(across) * count(later_plane)
        + count(first_moves & jnp.logical_not(to_later), second_moves, from_first),
    )
    for device, to_first in across:
        pl.when(to_first)(lambda device=device: signal(z_sem, device))
    pl.when(from_first)(lambda: signal(z_sem, first_from))

    links = Links(send_sem, recv_sem)

    WAYS = ((1, "f", 0), (-1, "b", 1))

    def amp(dz, dx, h=None, c=None):
        ref = col.at[occ_of(*zx(dz, dx), core if c is None else c)]
        return ref if h is None else ref.at[pl.ds(h * HALF, HALF)]

    def z_own():
        for late in range(2):
            for way, tag, h in WAYS:
                h = h if late == 0 else 1 - h
                links.send(("Tz", tag, h), amp(0, 0, h), at_zx(way, 0))

    def x_send(dz, h):
        for way, tag, _ in WAYS:
            links.send(("Tx", dz, tag, h), amp(dz, 0, h), at_zx(0, way))

    def x_own():
        for late in range(2):
            for way, tag, h in WAYS:
                h = h if late == 0 else 1 - h
                links.send(("Tx", 0, tag, h), amp(0, 0, h), at_zx(0, way))
        to_sib(0, 0)

    def z_on(late):
        for way, tag, h in WAYS:
            h = h if late == 0 else 1 - h
            links.recv(("Tz", tag, h), amp(-way, 0, h), at_zx(-way, 0))
            if late == 0:
                links.send(("Tzz", tag), amp(-way, 0, h), at_zx(way, 0))
            x_send(-way, h)
            if late == 1:
                to_sib(-way, 0)

    def z_far():
        for way, tag, h in WAYS:
            links.recv(("Tzz", tag), amp(2, 0, h), at_zx(-way, 0))
            x_send(2, h)
        to_sib(2, 0)

    def x_on(dz):
        for way, tag, h in WAYS:
            links.recv(("Tx", dz, tag, h), amp(dz, -way, h), at_zx(0, -way))
            links.send(("Txx", dz, tag), amp(dz, -way, h), at_zx(0, way))

    def x_rest(dz):
        for way, tag, h in WAYS:
            links.recv(("Tx", dz, tag, 1 - h), amp(dz, -way, 1 - h), at_zx(0, -way))
            to_sib(dz, -way)

    def x_far(dz):
        for way, tag, h in WAYS:
            links.recv(("Txx", dz, tag), amp(dz, 2, h), at_zx(0, -way))
        to_sib(dz, 2)

    def to_sib(dz, dx):
        links.send(("Ts", dz, dx), amp(dz, dx), sibling)

    def add_hole(dz, dx):
        links.recv(("Ts", dz, dx), amp(dz, dx, c=1 - core), sibling)
        zz, xx = zx(dz, dx)
        c = zz * NX + xx
        block = col[pl.ds(c * 2, 2)].reshape(2 * ROWS, COLS)
        ints_ = hole_ints[:, pl.ds(pl.multiple_of(c * 512, 512), 512)]
        total[...] += jnp.dot(ints_, block, preferred_element_type=jnp.float32)

    def ints(dz, dx, h=None, c=None):
        zz, xx = zx(dz, dx)
        ref = slab.at[(core if c is None else c) * 16 + zz * NX + xx]
        return ref if h is None else ref.at[pl.ds(h * HALF, HALF)]

    def p_z():
        for way, tag, h in WAYS:
            links.send(("pz", tag), ints(0, 0), at_zx(way, 0))

    def p_x(dz):
        for way, tag, h in WAYS:
            links.send(("px", dz, tag), ints(dz, 0), at_zx(0, way))
        links.send(("ps", dz, 0), ints(dz, 0), sibling)

    def p_z_on():
        for way, tag, h in WAYS:
            links.recv(("pz", tag), ints(-way, 0), at_zx(-way, 0))
            links.send(("pzz", tag), ints(-way, 0, h), at_zx(way, 0))
            p_x(-way)

    def p_z_far():
        for way, tag, h in WAYS:
            links.recv(("pzz", tag), ints(2, 0, h), at_zx(-way, 0))
        p_x(2)

    def p_x_on(dz):
        for way, tag, h in WAYS:
            links.recv(("px", dz, tag), ints(dz, -way), at_zx(0, -way))
            links.send(("pxx", dz, tag), ints(dz, -way, h), at_zx(0, way))
            links.send(("ps", dz, -way), ints(dz, -way), sibling)

    def p_x_far(dz):
        for way, tag, h in WAYS:
            links.recv(("pxx", dz, tag), ints(dz, 2, h), at_zx(0, -way))
        links.send(("ps", dz, 2), ints(dz, 2), sibling)

    def add_particle(dz, dx):
        links.recv(("ps", dz, dx), ints(dz, dx, c=1 - core), sibling)
        zz, xx = zx(dz, dx)
        p = zz * NX + xx
        k = lax.rem(zz // 2 + zl, 2) * NY + lax.rem(zz + y2, 2) * 4 + wrap(xx - yl, 4)
        block = jnp.concatenate([slab[p], slab[16 + p]], axis=1)
        total[...] += jnp.dot(row[k], block, preferred_element_type=jnp.float32)

    def strip(e, dy, h=None):
        ref = row.at[(zl if e == 0 else 1 - zl) * NY + wrap(y + dy, NY)]
        return ref if h is None else ref.at[pl.ds(h * HALF, HALF)]

    def y_send(e, hop):
        for way, tag, h in WAYS:
            if hop < 4:
                links.send(("y", e, hop, tag), strip(e, -way * (hop - 1)), at_y(way))
            else:
                links.send(("y", e, hop, tag), strip(e, -way * 3, h), at_y(way))

    def y_recv(e, hop):
        for way, tag, h in WAYS:
            if hop < 4:
                links.recv(("y", e, hop, tag), strip(e, -way * hop), at_y(-way))
            else:
                links.recv(("y", e, hop, tag), strip(e, 4, h), at_y(-way))

    def y_on(e, hop):
        y_recv(e, hop)
        y_send(e, hop + 1)

    def move(name, src, dst, to, come_from, moves, sem):
        def start():
            @pl.when(moves)
            def _():
                links.copy((name,), src, dst, to).start()

            @pl.when(jnp.logical_not(moves))
            def _():
                pltpu.make_async_copy(src, dst, sem).start()

        def arrive():
            @pl.when(moves)
            def _():
                links.copy((name,), src, dst, come_from).wait_recv()

            @pl.when(jnp.logical_not(moves))
            def _():
                pltpu.make_async_copy(src, dst, sem).wait()

        def leave():
            @pl.when(moves)
            def _():
                links.copy((name,), src, dst, to).wait_send()

        return start, arrive, leave

    first = move("1", part_hbm, moved, first_to, first_from, first_moves, load_sem.at[6])
    second_ = move("2", moved, ints(0, 0), second, second, second_moves, load_sem.at[7])

    def step(name, fn, *args, when=None):
        if when is None:
            fn(*args)
        else:
            pl.when(when)(lambda: fn(*args))

    step("first0", first[0], when=jnp.logical_not(to_later))
    step("x_own", x_own)
    step("e_y01", y_send, 0, 1, when=first_plane)
    step("e_x_on", x_on, 0, when=first_plane)
    step("e_y1", y_on, 0, 1, when=first_plane)
    step("e_x_rest", x_rest, 0, when=first_plane)
    step("e_x_far", x_far, 0, when=first_plane)
    step("z_sem", lambda: pl.semaphore_wait(z_sem, len(across) + count(to_later)), when=first_plane)
    step("first0", first[0], when=to_later)
    step("z_own", z_own)
    step("y01", y_send, 0, 1, when=later_plane)
    total[...] = jnp.zeros_like(total)
    step("x_on0", x_on, 0, when=later_plane)
    step("first_in", first[1])
    step("second", second_[0])
    step("y_on01", y_on, 0, 1, when=later_plane)
    step("x_rest0", x_rest, 0, when=later_plane)
    step("z_on0", z_on, 0)
    step("x_far0", x_far, 0, when=later_plane)
    step("pair", lambda: links.send(("ypair",), row.at[v], partner))
    step("z_on1", z_on, 1)
    step("y_on02", y_on, 0, 2)
    step("second_in", second_[1])
    step("p_z", p_z)
    step("p_x0", p_x, 0)
    step("x_on-1", x_on, -1)
    step("x_on1", x_on, 1)
    step("z_far", z_far)
    step("pair_recv", lambda: links.recv(("ypair",), strip(1, 0), partner))
    step("y11", y_send, 1, 1)
    step("load", loads[1].wait)
    step("h00", add_hole, 0, 0)
    step("h01", add_hole, 0, 1)
    step("h0-1", add_hole, 0, -1)
    step("x_rest-1", x_rest, -1)
    step("x_rest1", x_rest, 1)
    step("y_on03", y_on, 0, 3)
    step("p_z_on", p_z_on)
    step("p_x_on0", p_x_on, 0)
    step("x_far-1", x_far, -1)
    step("x_far1", x_far, 1)
    step("x_on2", x_on, 2)
    step("y_on11", y_on, 1, 1)
    step("p_z_far", p_z_far)
    step("h02", add_hole, 0, 2)
    step("h-10", add_hole, -1, 0)
    step("h10", add_hole, 1, 0)
    step("x_rest2", x_rest, 2)
    step("x_far2", x_far, 2)
    step("y_on12", y_on, 1, 2)
    step("p_x_on-1", p_x_on, -1)
    step("p_x_on1", p_x_on, 1)
    for dz, dx in ((-1, -1), (-1, 1), (1, -1), (1, 1), (2, 0)):
        step(f"h{dz}{dx}", add_hole, dz, dx)
    step("y_on13", y_on, 1, 3)
    step("p_x_far0", p_x_far, 0)
    step("p_x_on2", p_x_on, 2)
    for dz, dx in ((-1, 2), (1, 2), (2, -1), (2, 1), (2, 2)):
        step(f"h{dz}{dx}", add_hole, dz, dx)
    step("p_x_far-1", p_x_far, -1)
    step("p_x_far1", p_x_far, 1)
    step("y04", y_recv, 0, 4)
    step("y14", y_recv, 1, 4)
    step("p_x_far2", p_x_far, 2)
    for dz in (0, -1, 1, 2):
        for dx in (0, -1, 1, 2):
            step(f"p{dz}{dx}", add_particle, dz, dx)

    def finish():
        for load in loads[2:5]:
            load.wait()
        occ_col = jnp.transpose(jnp.broadcast_to(occ_ref[...], (TILE, ROWS)))
        for i in range(2):
            for j in range(2):
                rows, cols = pl.ds(i * TILE, TILE), pl.ds(j * TILE, TILE)
                keep = screen[i : i + 1, j : j + 1].astype(jnp.float32)
                a = amps[rows, cols].astype(jnp.float32)
                denom = virt_ref[:, cols] - occ_col[i * TILE : (i + 1) * TILE]
                ladders = total[rows, cols]
                res = keep * (direct[rows, cols].astype(jnp.float32) + ladders - denom * a)
                residual_ref[rows, cols] = res
                updated_ref[rows, cols] = (a + res / denom).astype(jnp.bfloat16)

    step("finish", finish)
    step("leave1", first[2])
    step("leave2", second_[2])
    step("drainT", links.drain, "T", col.at[pl.ds(0, 31)], sibling)
    step("drainy", links.drain, "y", row.at[pl.ds(0, 15)], sibling)
    step("drainp", links.drain, "p", slab.at[pl.ds(0, 31)], sibling)
    assert len(links.ids) <= N_COPIES


def on_device(amplitudes, screen, hole_ints, particle_ints, direct_ints, occ_energy, virt_energy):
    vmem, hbm = pl.BlockSpec(memory_space=pltpu.VMEM), pl.BlockSpec(memory_space=pltpu.HBM)
    return pl.pallas_call(
        kernel,
        out_shape=(
            jax.ShapeDtypeStruct((ROWS, COLS), jnp.float32),
            jax.ShapeDtypeStruct((ROWS, COLS), jnp.bfloat16),
        ),
        in_specs=[hbm] * 7,
        out_specs=(vmem, vmem),
        scratch_shapes=[
            pltpu.VMEM((ROWS, COLS), jnp.bfloat16),
            pltpu.VMEM((ROWS, COLS), jnp.bfloat16),
            pltpu.VMEM((ROWS, 8192), jnp.bfloat16),
            pltpu.VMEM((32, ROWS, COLS), jnp.bfloat16),
            pltpu.VMEM((16, ROWS, COLS), jnp.bfloat16),
            pltpu.VMEM((32, ROWS, TILE), jnp.bfloat16),
            pltpu.VMEM((ROWS, TILE), jnp.bfloat16),
            pltpu.VMEM((ROWS, COLS), jnp.float32),
            pltpu.VMEM((1, ROWS), jnp.float32),
            pltpu.VMEM((1, COLS), jnp.float32),
            pltpu.VMEM((2, 2), jnp.int32),
            pltpu.SemaphoreType.DMA((5,)),
            pltpu.SemaphoreType.DMA((N_COPIES,)),
            pltpu.SemaphoreType.DMA((8,)),
            pltpu.SemaphoreType.REGULAR,
        ],
        compiler_params=pltpu.CompilerParams(
            collective_id=0, has_side_effects=True, vmem_limit_bytes=62 * 2**20
        ),
        name="ladders",
    )(
        screen,
        amplitudes,
        hole_ints,
        particle_ints,
        direct_ints,
        occ_energy.reshape(1, ROWS),
        virt_energy.reshape(1, COLS),
    )


def solution(mesh):
    in_specs = (
        P("occ", "virt"),
        P("occ", "virt"),
        P("occ", None),
        P("virt", "occ"),
        P("occ", "virt"),
        P("occ"),
        P("virt"),
    )
    out_specs = (P("occ", "virt"), P("occ", "virt"))
    return jax.shard_map(
        on_device, mesh=mesh, in_specs=in_specs, out_specs=out_specs, check_vma=False
    )
```

```python
import math

import jax
import jax.numpy as jnp
from jax import lax
from jax.experimental import pallas as pl
from jax.experimental.pallas import tpu as pltpu
from jax.sharding import PartitionSpec as P

MESH = pl.DeviceIdType.MESH
NX, NZH, NY, NZL = 4, 4, 8, 2
ROWS, COLS, HALF, TILE = 256, 256, 128, 128


def wrap(a, n):
    return lax.rem(a + n, n)


class Links:
    KINDS = "TOqySRp12"
    ON_CORE_0 = "TOqy"

    def __init__(self, send_sem, recv_sem):
        self.send_sem, self.recv_sem = send_sem, recv_sem
        self.ids, self.sent = ({}, {}), {}

    def copy(self, name, src, dst, device):
        ids = self.ids[name[0][0] not in self.ON_CORE_0]
        n = ids.setdefault(name, len(ids))
        return pltpu.make_async_remote_copy(
            src_ref=src,
            dst_ref=dst,
            send_sem=self.send_sem.at[self.KINDS.index(name[0][0])],
            recv_sem=self.recv_sem.at[n],
            device_id=device,
            device_id_type=MESH,
        )

    def send(self, name, src, device, dst=None):
        self.copy(name, src, src if dst is None else dst, device).start()
        self.sent[name] = math.prod(src.shape)

    def recv(self, name, dst, device):
        self.copy(name, dst, dst, device).wait_recv()

    def drain(self, kind, everything, device):
        sent = sum(size for name, size in self.sent.items() if name[0][0] == kind)
        assert sent == math.prod(everything.shape)
        name = next(name for name in self.sent if name[0][0] == kind)
        self.copy(name, everything, everything, device).wait_send()


N_COPIES = 80


def kernel(
    screen_hbm,
    amps_hbm,
    hole_hbm,
    part_hbm,
    direct_hbm,
    occ_hbm,
    virt_hbm,
    residual_ref,
    updated_ref,
    amps,
    direct,
    hole_ints,
    col,
    row,
    slab,
    moved,
    total,
    occ_ref,
    virt_ref,
    screen,
    send_sem,
    recv_sem,
    load_sem,
):
    o, v = lax.axis_index("occ"), lax.axis_index("virt")
    core, chip = lax.rem(o, 2), o // 2
    x, zh = lax.rem(chip, NX), chip // NX
    zl, y = v // NY, lax.rem(v, NY)
    yl, y2 = lax.rem(y, 4), y // 4

    def occ_of(zh, x, core):
        return (zh * NX + x) * 2 + core

    def zx(dz, dx):
        return wrap(zh + dz, NZH), wrap(x + dx, NX)

    def at_zx(dz, dx):
        return (occ_of(*zx(dz, dx), core), v)

    def at_y(dy):
        return (o, zl * NY + wrap(y + dy, NY))

    def flipped(zh, hi, lo):
        return lax.rem(zh // 2 + hi, 2) * 2 + lax.rem(zh + lo, 2)

    sibling = (occ_of(zh, x, 1 - core), v)
    partner = (o, (1 - zl) * NY + y)
    zh_1 = flipped(zh, zl, y2)
    first_to = (occ_of(zh_1, wrap(x + yl, NX), 1), v)
    first_from = [(occ_of(zh_1, wrap(x - yl, NX), c), v) for c in range(2)]
    first_moves = v != 0
    v_2 = lax.rem(zh // 2 + zl, 2) * NY + lax.rem(zh + y2, 2) * 4 + wrap(x - yl, 4)
    second = (o, v_2)
    second_moves = v_2 != v
    lead, other = core == 0, core == 1

    def signal(sem, device):
        pl.semaphore_signal(sem, inc=1, device_id=device, device_id_type=MESH)

    def count(*flags):
        return sum(flag.astype(jnp.int32) for flag in flags)

    loads = [
        pltpu.make_async_copy(src, dst, load_sem.at[n])
        for n, (src, dst) in enumerate(
            (
                (amps_hbm, amps),
                (hole_hbm, hole_ints),
                (direct_hbm, direct),
                (occ_hbm, occ_ref),
                (virt_hbm, virt_ref),
                (screen_hbm, screen),
            )
        )
    ]
    loads[0].start()
    loads[5].start()

    barrier = pltpu.get_barrier_semaphore()
    for device in first_from:
        pl.when(other & first_moves)(lambda device=device: signal(barrier, device))
    pl.when(other & second_moves)(lambda: signal(barrier, second))
    for device in (at_zx(1, 0), at_zx(-1, 0), at_zx(0, 1), at_zx(0, -1), sibling):
        signal(barrier, device)
    for device in (at_y(1), at_y(-1), partner):
        pl.when(lead)(lambda device=device: signal(barrier, device))

    for load in loads[1:5]:
        load.start()
    loads[0].wait()
    loads[5].wait()
    for i in range(2):
        for j in range(2):
            rows, cols = pl.ds(i * TILE, TILE), pl.ds(j * TILE, TILE)
            keep = screen[i : i + 1, j : j + 1].astype(jnp.float32)
            tile = (amps[rows, cols].astype(jnp.float32) * keep).astype(jnp.bfloat16)
            col[o, rows, cols] = tile
            row[v * 2 + core, rows, cols] = tile

    pl.semaphore_wait(barrier, 5 + 3 * count(lead) + count(first_moves, other & second_moves))

    links = Links(send_sem, recv_sem)

    WAYS = ((1, "f", 0), (-1, "b", 1))

    def amp(dz, dx, h=None):
        zz, xx = zx(dz, dx)
        c = (zz * NX + xx) * 2
        return col.at[pl.ds(c, 2)] if h is None else col.at[c + h]


    def to_sib(dz, dx):
        links.send(("S", dz, dx), amp(dz, dx), sibling)

    def z_send(way, tag, h):
        links.send(("Tz", tag, h), amp(0, 0, h), at_zx(way, 0))

    def x_send(dz, h):
        for way, tag, _ in WAYS:
            links.send(("Tx", dz, tag, h), amp(dz, 0, h), at_zx(0, way))

    def x0_send(way, tag, h):
        links.send(("Tx", 0, tag, h), amp(0, 0, h), at_zx(0, way))

    def x_recv(dz, way, tag, h):
        links.recv(("Tx", dz, tag, h), amp(dz, -way, h), at_zx(0, -way))

    def x_pass(dz, way, tag, h):
        links.send(("Txx", dz, tag), amp(dz, -way, h), at_zx(0, way))

    def z_first():
        for way, tag, h in WAYS:
            links.recv(("Tz", tag, h), amp(-way, 0, h), at_zx(-way, 0))
            links.send(("Tzz", tag), amp(-way, 0, h), at_zx(way, 0))
            x_send(-way, h)

    def z_rest():
        for way, tag, h in WAYS:
            links.recv(("Tz", tag, 1 - h), amp(-way, 0, 1 - h), at_zx(-way, 0))
            x_send(-way, 1 - h)
        for way, _, _ in WAYS:
            to_sib(-way, 0)

    def z_far():
        for way, tag, h in WAYS:
            links.recv(("Tzz", tag), amp(2, 0, h), at_zx(-way, 0))
        for way, tag, h in WAYS:
            links.send(("Tx", 2, tag), amp(2, 0), at_zx(0, way))
        to_sib(2, 0)

    def x0_first():
        for way, tag, h in WAYS:
            x_recv(0, way, tag, h)
            x_pass(0, way, tag, h)

    def x0_rest():
        for way, tag, h in WAYS:
            x_recv(0, way, tag, 1 - h)
            to_sib(0, -way)

    def x1_first():
        for dz, early in ((-1, 0), (1, 1)):
            for way, tag, h in WAYS:
                x_recv(dz, way, tag, early)
                if h == early:
                    x_pass(dz, way, tag, h)

    def x1_rest():
        for dz, early in ((-1, 0), (1, 1)):
            for way, tag, h in WAYS:
                x_recv(dz, way, tag, 1 - early)
                if h != early:
                    x_pass(dz, way, tag, h)
            for way, _, _ in WAYS:
                to_sib(dz, -way)

    def x2_all():
        for way, tag, h in WAYS:
            links.recv(("Tx", 2, tag), amp(2, -way), at_zx(0, -way))
            x_pass(2, way, tag, h)
            to_sib(2, -way)

    def x_far(dz):
        for way, tag, h in WAYS:
            links.recv(("Txx", dz, tag), amp(dz, 2, h), at_zx(0, -way))
        to_sib(dz, 2)


    def turned(a, b, h):
        return (a, b) if h == 0 else (b, a)

    def ints(dz, dx, h=None, part=None):
        zz, xx = zx(dz, dx)
        p = (zz * NX + xx) * 2
        ref = slab.at[pl.ds(p, 2)] if h is None else slab.at[p + h]
        return ref if part is None else ref.at[pl.ds(part * HALF, HALF)]

    def p_send(a):
        for half in range(2):
            for way, tag, _ in WAYS:
                links.send(("pb", a, half, tag), ints(*turned(a, 0, half), half), at_zx(*turned(0, way, half)))

    def p_own():
        for half in range(2):
            for way, tag, _ in WAYS:
                links.send(("pa", half, tag), ints(0, 0, half), at_zx(*turned(way, 0, half)))
        p_send(0)

    def pa_all():
        for half in range(2):
            for way, tag, h in WAYS:
                here = turned(-way, 0, half)
                links.recv(("pa", half, tag), ints(*here, half), at_zx(*here))
                links.send(("paa", half, tag), ints(*here, half, h), at_zx(*turned(way, 0, half)))
        for way, _, _ in WAYS:
            p_send(-way)

    def pa_far():
        for half in range(2):
            for way, tag, h in WAYS:
                links.recv(
                    ("paa", half, tag), ints(*turned(2, 0, half), half, h), at_zx(*turned(-way, 0, half))
                )
        p_send(2)

    def pb_all(a):
        for half in range(2):
            for way, tag, h in WAYS:
                here = turned(a, -way, half)
                links.recv(("pb", a, half, tag), ints(*here, half), at_zx(*turned(0, -way, half)))
                links.send(("pbb", a, half, tag), ints(*here, half, h), at_zx(*turned(0, way, half)))

    def pb_far(a):
        for half in range(2):
            for way, tag, h in WAYS:
                links.recv(
                    ("pbb", a, half, tag),
                    ints(*turned(a, 2, half), half, h),
                    at_zx(*turned(0, -way, half)),
                )

    def p_sibs(*places):
        for place in places:
            links.send(("q",) + place, ints(*place), sibling)

    def strip(e, dy, h=None):
        k = ((zl if e == 0 else 1 - zl) * NY + wrap(y + dy, NY)) * 2
        return row.at[pl.ds(k, 2)] if h is None else row.at[k + h]

    def y_send(e, hop, half):
        for way, tag, h in WAYS:
            if hop < 4 or h == half:
                dst = strip(e, -way * (hop - 1), half)
                src = amp(0, 0, half) if (e, hop) == (0, 1) else dst
                links.send(("y", e, hop, tag, half), src, at_y(way), dst)

    def y_on(e, hop, half):
        for way, tag, h in WAYS:
            if hop < 4 or h == half:
                links.recv(("y", e, hop, tag, half), strip(e, -way * hop, half), at_y(-way))
        if hop < 4:
            y_send(e, hop + 1, half)
        if half == 1:
            for dy in (hop, -hop) if hop < 4 else (4,):
                row_sib(e, dy)

    def row_sib(e, dy):
        links.send(("R", e, dy), strip(e, dy, 1), sibling)

    def pair_send(half):
        links.send(("ypair", half), amp(0, 0, half), partner, strip(0, 0, half))

    def pair_on(half):
        links.recv(("ypair", half), strip(1, 0, half), partner)
        y_send(1, 1, half)
        if half == 1:
            row_sib(1, 0)


    def add_hole(dz, dx, block):
        zz, xx = zx(dz, dx)
        ints_ = hole_ints[:, pl.ds(pl.multiple_of((zz * NX + xx) * 512, 512), 512)]
        total[...] += jnp.dot(
            ints_, block[...].reshape(2 * ROWS, COLS), preferred_element_type=jnp.float32
        )

    def take_holes(*places):
        for place in places:
            add_hole(*place, amp(*place))

    def get_holes(*places):
        for place in places:
            if place != (0, 0):
                links.recv(("S",) + place, amp(*place), sibling)
            add_hole(*place, amp(*place))

    def add_particle(dz, dx):
        zz, xx = zx(dz, dx)
        p = (zz * NX + xx) * 2
        k = lax.rem(zz // 2 + zl, 2) * NY + lax.rem(zz + y2, 2) * 4 + wrap(xx - yl, 4)
        block = jnp.concatenate([slab[p], slab[p + 1]], axis=1)
        total[...] += jnp.dot(row[k * 2 + core], block, preferred_element_type=jnp.float32)

    def take_particles(*places):
        for place in places:
            add_particle(*place)

    def get_rows():
        for e in range(2):
            for dy in range(e == 0, NY):
                links.recv(("R", e, dy if dy <= 4 else dy - NY), strip(e, dy, 1), sibling)

    def get_particles(*places):
        for place in places:
            links.recv(("q",) + place, ints(*place), sibling)
            add_particle(*place)


    def first():
        pl.when(lead)(lambda: links.send(("1", 0), part_hbm, first_to, moved.at[0]))
        pl.when(other & first_moves)(lambda: links.send(("1", 1), part_hbm, first_to, moved.at[1]))
        pl.when(other & jnp.logical_not(first_moves))(
            lambda: pltpu.make_async_copy(part_hbm, moved.at[1], load_sem.at[6]).start()
        )

    def first_in():
        links.recv(("1", 0), moved.at[0], first_from[0])
        pl.when(first_moves)(lambda: links.recv(("1", 1), moved.at[1], first_from[1]))
        pl.when(jnp.logical_not(first_moves))(
            lambda: pltpu.make_async_copy(part_hbm, moved.at[1], load_sem.at[6]).wait()
        )

    def second_out():
        pl.when(second_moves)(lambda: links.send(("2",), moved, second, ints(0, 0)))
        pl.when(jnp.logical_not(second_moves))(
            lambda: pltpu.make_async_copy(moved, ints(0, 0), load_sem.at[7]).start()
        )

    def second_in():
        pl.when(second_moves)(lambda: links.recv(("2",), ints(0, 0), second))
        pl.when(jnp.logical_not(second_moves))(
            lambda: pltpu.make_async_copy(moved, ints(0, 0), load_sem.at[7]).wait()
        )

    def step(name, fn, *args, when=None):
        if when is None:
            fn(*args)
        else:
            pl.when(when)(lambda: fn(*args))

    total[...] = jnp.zeros_like(total)

    def program_0():
        step("first", first)
        step("x0_send", x0_send, 1, "f", 0)
        step("z_send", z_send, 1, "f", 0)
        step("y_own0", y_send, 0, 1, 0)
        step("pair0", pair_send, 0)
        step("own_sib", lambda: links.send(("S",), amp(0, 0, 0), sibling))
        step("own_sib_in", lambda: links.recv(("O",), amp(0, 0, 1), sibling))
        step("x0_send", x0_send, -1, "b", 1)
        step("z_send", z_send, -1, "b", 1)
        step("x0_send", x0_send, 1, "f", 1)
        step("z_send", z_send, 1, "f", 1)
        step("x0_send", x0_send, -1, "b", 0)
        step("z_send", z_send, -1, "b", 0)
        step("pair1", pair_send, 1)
        step("y_own1", y_send, 0, 1, 1)
        step("y01a", y_on, 0, 1, 0)
        step("x0", x0_first)
        step("y01b", y_on, 0, 1, 1)
        step("x0r", x0_rest)
        step("pair0", pair_on, 0)
        step("z_first", z_first)
        step("y02a", y_on, 0, 2, 0)
        step("pair1", pair_on, 1)
        step("y02b", y_on, 0, 2, 1)
        step("xf0", x_far, 0)
        step("z_rest", z_rest)
        step("y11a", y_on, 1, 1, 0)
        step("x1", x1_first)
        step("y03a", y_on, 0, 3, 0)
        step("load", loads[1].wait)
        step("h0", take_holes, (0, 0), (0, -1), (0, 1), (0, 2))
        step("y11b", y_on, 1, 1, 1)
        step("y03b", y_on, 0, 3, 1)
        step("z_far", z_far)
        step("y12a", y_on, 1, 2, 0)
        step("x1r", x1_rest)
        step("h1", take_holes, (-1, 0), (1, 0), (2, 0))
        step("y12b", y_on, 1, 2, 1)
        step("y04", y_on, 0, 4, 0)
        step("y04", y_on, 0, 4, 1)
        step("h2", take_holes, (-1, -1), (-1, 1), (1, -1), (1, 1))
        step("y13a", y_on, 1, 3, 0)
        step("x2", x2_all)
        step("y13b", y_on, 1, 3, 1)
        step("h2", take_holes, (2, -1), (2, 1))
        step("xf-1", x_far, -1)
        step("xf1", x_far, 1)
        step("h3", take_holes, (-1, 2), (1, 2))
        step("y14", y_on, 1, 4, 0)
        step("y14", y_on, 1, 4, 1)
        step("p0", get_particles, (0, 0), (-1, 0), (1, 0), (0, -1), (0, 1), (0, 2), (2, 0))
        step("xf2", x_far, 2)
        step("p1", get_particles, (-1, -1), (-1, 1), (1, -1), (1, 1))
        step("h3", take_holes, (2, 2))
        step("p2", get_particles, (-1, 2), (1, 2), (2, -1), (2, 1))
        step("p3", get_particles, (2, 2))

    def program_1():
        step("first", first)
        step("own_sib", lambda: links.send(("O",), amp(0, 0, 1), sibling))
        step("own_sib_in", lambda: links.recv(("S",), amp(0, 0, 0), sibling))
        step("first_in", first_in)
        step("second", second_out)
        step("load", loads[1].wait)
        step("h0", get_holes, (0, 0), (0, -1), (0, 1), (0, 2))
        step("second_in", second_in)
        step("p_own", p_own)
        step("ps0", p_sibs, (0, 0))
        step("h1", get_holes, (-1, 0), (1, 0))
        step("pa", pa_all)
        step("pb0", pb_all, 0)
        step("ps1", p_sibs, (0, 1), (0, -1), (1, 0), (-1, 0))
        step("h1", get_holes, (2, 0))
        step("pa_far", pa_far)
        step("pbb0", pb_far, 0)
        step("ps2", p_sibs, (0, 2), (2, 0))
        step("pb-1", pb_all, -1)
        step("pb1", pb_all, 1)
        step("ps3", p_sibs, (-1, -1), (-1, 1), (1, -1), (1, 1))
        step("h2", get_holes, (-1, -1), (-1, 1), (1, -1), (1, 1))
        step("pb2", pb_all, 2)
        step("pbb-1", pb_far, -1)
        step("pbb1", pb_far, 1)
        step("ps4", p_sibs, (-1, 2), (1, 2), (2, -1), (2, 1))
        step("h3", get_holes, (2, -1), (2, 1))
        step("pbb2", pb_far, 2)
        step("ps5", p_sibs, (2, 2))
        step("h3", get_holes, (-1, 2), (1, 2))
        step("rows", get_rows)
        step("p0", take_particles, (0, 0), (-1, 0), (1, 0), (0, -1), (0, 1), (0, 2), (2, 0))
        step("p1", take_particles, (-1, -1), (-1, 1), (1, -1), (1, 1))
        step("p2", take_particles, (-1, 2), (1, 2), (2, -1), (2, 1), (2, 2))
        step("h3", get_holes, (2, 2))

    def drain_0():
        links.drain("T", col.at[pl.ds(0, 30)], sibling)
        links.drain("S", col.at[pl.ds(0, 31)], sibling)
        links.drain("y", row.at[pl.ds(0, 30)], sibling)
        links.drain("R", row.at[pl.ds(0, 15)], sibling)

    def drain_1():
        links.drain("O", col.at[pl.ds(0, 1)], sibling)
        links.drain("p", slab.at[pl.ds(0, 30)], sibling)
        links.drain("q", slab, sibling)
        pl.when(second_moves)(lambda: links.copy(("2",), moved, moved, sibling).wait_send())

    pl.when(lead)(program_0)
    pl.when(other)(program_1)

    def finish():
        for load in loads[2:5]:
            load.wait()
        occ_col = jnp.transpose(jnp.broadcast_to(occ_ref[...], (TILE, ROWS)))
        for i in range(2):
            for j in range(2):
                rows, cols = pl.ds(i * TILE, TILE), pl.ds(j * TILE, TILE)
                keep = screen[i : i + 1, j : j + 1].astype(jnp.float32)
                a = amps[rows, cols].astype(jnp.float32)
                denom = virt_ref[:, cols] - occ_col[i * TILE : (i + 1) * TILE]
                ladders = total[rows, cols]
                res = keep * (direct[rows, cols].astype(jnp.float32) + ladders - denom * a)
                residual_ref[rows, cols] = res
                updated_ref[rows, cols] = (a + res / denom).astype(jnp.bfloat16)

    step("finish", finish)
    pl.when(lead)(drain_0)
    pl.when(other)(drain_1)
    pl.when(lead | first_moves)(lambda: links.copy(("1", 0), moved.at[0], moved.at[0], sibling).wait_send())
    assert max(map(len, links.ids)) <= N_COPIES


def on_device(amplitudes, screen, hole_ints, particle_ints, direct_ints, occ_energy, virt_energy):
    vmem, hbm = pl.BlockSpec(memory_space=pltpu.VMEM), pl.BlockSpec(memory_space=pltpu.HBM)
    return pl.pallas_call(
        kernel,
        out_shape=(
            jax.ShapeDtypeStruct((ROWS, COLS), jnp.float32),
            jax.ShapeDtypeStruct((ROWS, COLS), jnp.bfloat16),
        ),
        in_specs=[hbm] * 7,
        out_specs=(vmem, vmem),
        scratch_shapes=[
            pltpu.VMEM((ROWS, COLS), jnp.bfloat16),
            pltpu.VMEM((ROWS, COLS), jnp.bfloat16),
            pltpu.VMEM((ROWS, 8192), jnp.bfloat16),
            pltpu.VMEM((32, ROWS, COLS), jnp.bfloat16),
            pltpu.VMEM((32, ROWS, COLS), jnp.bfloat16),
            pltpu.VMEM((32, ROWS, TILE), jnp.bfloat16),
            pltpu.VMEM((2, ROWS, TILE), jnp.bfloat16),
            pltpu.VMEM((ROWS, COLS), jnp.float32),
            pltpu.VMEM((1, ROWS), jnp.float32),
            pltpu.VMEM((1, COLS), jnp.float32),
            pltpu.VMEM((2, 2), jnp.int32),
            pltpu.SemaphoreType.DMA((9,)),
            pltpu.SemaphoreType.DMA((N_COPIES,)),
            pltpu.SemaphoreType.DMA((8,)),
        ],
        compiler_params=pltpu.CompilerParams(
            collective_id=0, has_side_effects=True, vmem_limit_bytes=62 * 2**20
        ),
        name="ladders",
    )(
        screen,
        amplitudes,
        hole_ints,
        particle_ints,
        direct_ints,
        occ_energy.reshape(1, ROWS),
        virt_energy.reshape(1, COLS),
    )


def solution(mesh):
    in_specs = (
        P("occ", "virt"),
        P("occ", "virt"),
        P("occ", None),
        P("virt", "occ"),
        P("occ", "virt"),
        P("occ"),
        P("virt"),
    )
    out_specs = (P("occ", "virt"), P("occ", "virt"))
    return jax.shard_map(
        on_device, mesh=mesh, in_specs=in_specs, out_specs=out_specs, check_vma=False
    )
```

```python
import math

import jax
import jax.numpy as jnp
from jax import lax
from jax.experimental import pallas as pl
from jax.experimental.pallas import tpu as pltpu
from jax.sharding import PartitionSpec as P

MESH = pl.DeviceIdType.MESH
NX, NZH, NY, NZL = 4, 4, 8, 2
ROWS, COLS, HALF, TILE = 256, 256, 128, 128


def wrap(a, n):
    return lax.rem(a + n, n)


class Links:
    KINDS = "TOqySRp12"
    ON_CORE_0 = "TOqy"

    def __init__(self, send_sem, recv_sem):
        self.send_sem, self.recv_sem = send_sem, recv_sem
        self.ids, self.sent = ({}, {}), {}

    def copy(self, name, src, dst, device):
        ids = self.ids[name[0][0] not in self.ON_CORE_0]
        n = ids.setdefault(name, len(ids))
        return pltpu.make_async_remote_copy(
            src_ref=src,
            dst_ref=dst,
            send_sem=self.send_sem.at[self.KINDS.index(name[0][0])],
            recv_sem=self.recv_sem.at[n],
            device_id=device,
            device_id_type=MESH,
        )

    def send(self, name, src, device, dst=None):
        self.copy(name, src, src if dst is None else dst, device).start()
        self.sent[name] = math.prod(src.shape)

    def recv(self, name, dst, device):
        self.copy(name, dst, dst, device).wait_recv()

    def drain(self, kind, everything, device):
        sent = sum(size for name, size in self.sent.items() if name[0][0] == kind)
        assert sent == math.prod(everything.shape)
        name = next(name for name in self.sent if name[0][0] == kind)
        self.copy(name, everything, everything, device).wait_send()


N_COPIES = 80


def kernel(
    screen_hbm,
    amps_hbm,
    hole_hbm,
    part_hbm,
    direct_hbm,
    occ_hbm,
    virt_hbm,
    step_ref,
    amps,
    direct,
    hole_ints,
    col,
    row,
    slab,
    moved,
    total,
    occ_ref,
    virt_ref,
    screen,
    send_sem,
    recv_sem,
    load_sem,
):
    o, v = lax.axis_index("occ"), lax.axis_index("virt")
    core, chip = lax.rem(o, 2), o // 2
    x, zh = lax.rem(chip, NX), chip // NX
    zl, y = v // NY, lax.rem(v, NY)
    yl, y2 = lax.rem(y, 4), y // 4

    def occ_of(zh, x, core):
        return (zh * NX + x) * 2 + core

    def zx(dz, dx):
        return wrap(zh + dz, NZH), wrap(x + dx, NX)

    def at_zx(dz, dx):
        return (occ_of(*zx(dz, dx), core), v)

    def at_y(dy):
        return (o, zl * NY + wrap(y + dy, NY))

    def flipped(zh, hi, lo):
        return lax.rem(zh // 2 + hi, 2) * 2 + lax.rem(zh + lo, 2)

    sibling = (occ_of(zh, x, 1 - core), v)
    partner = (o, (1 - zl) * NY + y)
    zh_1 = flipped(zh, zl, y2)
    first_to = (occ_of(zh_1, wrap(x + yl, NX), 1), v)
    first_from = [(occ_of(zh_1, wrap(x - yl, NX), c), v) for c in range(2)]
    first_moves = v != 0
    v_2 = lax.rem(zh // 2 + zl, 2) * NY + lax.rem(zh + y2, 2) * 4 + wrap(x - yl, 4)
    second = (o, v_2)
    second_moves = v_2 != v
    lead, other = core == 0, core == 1

    def signal(sem, device):
        pl.semaphore_signal(sem, inc=1, device_id=device, device_id_type=MESH)

    def count(*flags):
        return sum(flag.astype(jnp.int32) for flag in flags)

    loads = [
        pltpu.make_async_copy(src, dst, load_sem.at[n])
        for n, (src, dst) in enumerate(
            (
                (amps_hbm, amps),
                (hole_hbm, hole_ints),
                (direct_hbm, direct),
                (occ_hbm, occ_ref),
                (virt_hbm, virt_ref),
                (screen_hbm, screen),
            )
        )
    ]
    loads[0].start()
    loads[5].start()

    barrier = pltpu.get_barrier_semaphore()
    for device in first_from:
        pl.when(other & first_moves)(lambda device=device: signal(barrier, device))
    pl.when(other & second_moves)(lambda: signal(barrier, second))
    for device in (at_zx(1, 0), at_zx(-1, 0), at_zx(0, 1), at_zx(0, -1), sibling):
        signal(barrier, device)
    for device in (at_y(1), at_y(-1), partner):
        pl.when(lead)(lambda device=device: signal(barrier, device))

    for load in loads[1:5]:
        load.start()
    loads[0].wait()
    loads[5].wait()
    for i in range(2):
        for j in range(2):
            rows, cols = pl.ds(i * TILE, TILE), pl.ds(j * TILE, TILE)
            keep = screen[i : i + 1, j : j + 1].astype(jnp.float32)
            tile = (amps[rows, cols].astype(jnp.float32) * keep).astype(jnp.bfloat16)
            col[o, rows, cols] = tile
            row[v * 2 + core, rows, cols] = tile

    pl.semaphore_wait(barrier, 5 + 3 * count(lead) + count(first_moves, other & second_moves))

    links = Links(send_sem, recv_sem)

    WAYS = ((1, "f", 0), (-1, "b", 1))

    def amp(dz, dx, h=None):
        zz, xx = zx(dz, dx)
        c = (zz * NX + xx) * 2
        return col.at[pl.ds(c, 2)] if h is None else col.at[c + h]


    def to_sib(dz, dx):
        links.send(("S", dz, dx), amp(dz, dx), sibling)

    def z_send(way, tag, h):
        links.send(("Tz", tag, h), amp(0, 0, h), at_zx(way, 0))

    def x_send(dz, h):
        for way, tag, _ in WAYS:
            links.send(("Tx", dz, tag, h), amp(dz, 0, h), at_zx(0, way))

    def x0_send(way, tag, h):
        links.send(("Tx", 0, tag, h), amp(0, 0, h), at_zx(0, way))

    def x_recv(dz, way, tag, h):
        links.recv(("Tx", dz, tag, h), amp(dz, -way, h), at_zx(0, -way))

    def x_pass(dz, way, tag, h):
        links.send(("Txx", dz, tag), amp(dz, -way, h), at_zx(0, way))

    def z_first():
        for way, tag, h in WAYS:
            links.recv(("Tz", tag, h), amp(-way, 0, h), at_zx(-way, 0))
            links.send(("Tzz", tag), amp(-way, 0, h), at_zx(way, 0))
            x_send(-way, h)

    def z_rest():
        for way, tag, h in WAYS:
            links.recv(("Tz", tag, 1 - h), amp(-way, 0, 1 - h), at_zx(-way, 0))
            x_send(-way, 1 - h)
        for way, _, _ in WAYS:
            to_sib(-way, 0)

    def z_far():
        for way, tag, h in WAYS:
            links.recv(("Tzz", tag), amp(2, 0, h), at_zx(-way, 0))
        for way, tag, h in WAYS:
            links.send(("Tx", 2, tag), amp(2, 0), at_zx(0, way))
        to_sib(2, 0)

    def x0_first():
        for way, tag, h in WAYS:
            x_recv(0, way, tag, h)
            x_pass(0, way, tag, h)

    def x0_rest():
        for way, tag, h in WAYS:
            x_recv(0, way, tag, 1 - h)
            to_sib(0, -way)

    def x1_first():
        for dz, early in ((-1, 0), (1, 1)):
            for way, tag, h in WAYS:
                x_recv(dz, way, tag, early)
                if h == early:
                    x_pass(dz, way, tag, h)

    def x1_rest():
        for dz, early in ((-1, 0), (1, 1)):
            for way, tag, h in WAYS:
                x_recv(dz, way, tag, 1 - early)
                if h != early:
                    x_pass(dz, way, tag, h)
            for way, _, _ in WAYS:
                to_sib(dz, -way)

    def x2_all():
        for way, tag, h in WAYS:
            links.recv(("Tx", 2, tag), amp(2, -way), at_zx(0, -way))
            x_pass(2, way, tag, h)
            to_sib(2, -way)

    def x_far(dz):
        for way, tag, h in WAYS:
            links.recv(("Txx", dz, tag), amp(dz, 2, h), at_zx(0, -way))
        to_sib(dz, 2)


    def turned(a, b, h):
        return (a, b) if h == 0 else (b, a)

    def ints(dz, dx, h=None, part=None):
        zz, xx = zx(dz, dx)
        p = (zz * NX + xx) * 2
        ref = slab.at[pl.ds(p, 2)] if h is None else slab.at[p + h]
        return ref if part is None else ref.at[pl.ds(part * HALF, HALF)]

    def p_send(a):
        for half in range(2):
            for way, tag, _ in WAYS:
                links.send(("pb", a, half, tag), ints(*turned(a, 0, half), half), at_zx(*turned(0, way, half)))

    def p_own():
        for half in range(2):
            for way, tag, _ in WAYS:
                links.send(("pa", half, tag), ints(0, 0, half), at_zx(*turned(way, 0, half)))
        p_send(0)

    def pa_all():
        for half in range(2):
            for way, tag, h in WAYS:
                here = turned(-way, 0, half)
                links.recv(("pa", half, tag), ints(*here, half), at_zx(*here))
                links.send(("paa", half, tag), ints(*here, half, h), at_zx(*turned(way, 0, half)))
        for way, _, _ in WAYS:
            p_send(-way)

    def pa_far():
        for half in range(2):
            for way, tag, h in WAYS:
                links.recv(
                    ("paa", half, tag), ints(*turned(2, 0, half), half, h), at_zx(*turned(-way, 0, half))
                )
        p_send(2)

    def pb_all(a):
        for half in range(2):
            for way, tag, h in WAYS:
                here = turned(a, -way, half)
                links.recv(("pb", a, half, tag), ints(*here, half), at_zx(*turned(0, -way, half)))
                links.send(("pbb", a, half, tag), ints(*here, half, h), at_zx(*turned(0, way, half)))

    def pb_far(a):
        for half in range(2):
            for way, tag, h in WAYS:
                links.recv(
                    ("pbb", a, half, tag),
                    ints(*turned(a, 2, half), half, h),
                    at_zx(*turned(0, -way, half)),
                )

    def p_sibs(*places):
        for place in places:
            links.send(("q",) + place, ints(*place), sibling)

    def strip(e, dy, h=None):
        k = ((zl if e == 0 else 1 - zl) * NY + wrap(y + dy, NY)) * 2
        return row.at[pl.ds(k, 2)] if h is None else row.at[k + h]

    def y_send(e, hop, half):
        for way, tag, h in WAYS:
            if hop < 4 or h == half:
                dst = strip(e, -way * (hop - 1), half)
                src = amp(0, 0, half) if (e, hop) == (0, 1) else dst
                links.send(("y", e, hop, tag, half), src, at_y(way), dst)

    def y_on(e, hop, half):
        for way, tag, h in WAYS:
            if hop < 4 or h == half:
                links.recv(("y", e, hop, tag, half), strip(e, -way * hop, half), at_y(-way))
        if hop < 4:
            y_send(e, hop + 1, half)
        if half == 1:
            for dy in (hop, -hop) if hop < 4 else (4,):
                row_sib(e, dy)

    def row_sib(e, dy):
        links.send(("R", e, dy), strip(e, dy, 1), sibling)

    def pair_send(half):
        links.send(("ypair", half), amp(0, 0, half), partner, strip(0, 0, half))

    def pair_on(half):
        links.recv(("ypair", half), strip(1, 0, half), partner)
        y_send(1, 1, half)
        if half == 1:
            row_sib(1, 0)


    def add_hole(dz, dx, block):
        zz, xx = zx(dz, dx)
        ints_ = hole_ints[:, pl.ds(pl.multiple_of((zz * NX + xx) * 512, 512), 512)]
        total[...] += jnp.dot(
            ints_, block[...].reshape(2 * ROWS, COLS), preferred_element_type=jnp.float32
        )

    def take_holes(*places):
        for place in places:
            add_hole(*place, amp(*place))

    def get_holes(*places):
        for place in places:
            if place != (0, 0):
                links.recv(("S",) + place, amp(*place), sibling)
            add_hole(*place, amp(*place))

    def add_particles(places):
        rows, blocks = [], []
        for dz, dx in places:
            zz, xx = zx(dz, dx)
            p = (zz * NX + xx) * 2
            k = lax.rem(zz // 2 + zl, 2) * NY + lax.rem(zz + y2, 2) * 4 + wrap(xx - yl, 4)
            rows.append(row[k * 2 + core])
            blocks.append(jnp.concatenate([slab[p], slab[p + 1]], axis=1))
        total[...] += jnp.dot(
            jnp.concatenate(rows, axis=1),
            jnp.concatenate(blocks, axis=0),
            preferred_element_type=jnp.float32,
        )

    def take_particles(*places):
        for n in range(0, len(places), 4):
            add_particles(places[n : n + 4])

    def get_rows():
        for e in range(2):
            for dy in range(e == 0, NY):
                links.recv(("R", e, dy if dy <= 4 else dy - NY), strip(e, dy, 1), sibling)

    def get_particles(*places):
        for place in places:
            links.recv(("q",) + place, ints(*place), sibling)
        take_particles(*places)


    def first():
        pl.when(lead)(lambda: links.send(("1", 0), part_hbm, first_to, moved.at[0]))
        pl.when(other & first_moves)(lambda: links.send(("1", 1), part_hbm, first_to, moved.at[1]))
        pl.when(other & jnp.logical_not(first_moves))(
            lambda: pltpu.make_async_copy(part_hbm, moved.at[1], load_sem.at[6]).start()
        )

    def first_in():
        links.recv(("1", 0), moved.at[0], first_from[0])
        pl.when(first_moves)(lambda: links.recv(("1", 1), moved.at[1], first_from[1]))
        pl.when(jnp.logical_not(first_moves))(
            lambda: pltpu.make_async_copy(part_hbm, moved.at[1], load_sem.at[6]).wait()
        )

    def second_out():
        pl.when(second_moves)(lambda: links.send(("2",), moved, second, ints(0, 0)))
        pl.when(jnp.logical_not(second_moves))(
            lambda: pltpu.make_async_copy(moved, ints(0, 0), load_sem.at[7]).start()
        )

    def second_in():
        pl.when(second_moves)(lambda: links.recv(("2",), ints(0, 0), second))
        pl.when(jnp.logical_not(second_moves))(
            lambda: pltpu.make_async_copy(moved, ints(0, 0), load_sem.at[7]).wait()
        )

    def step(name, fn, *args, when=None):
        if when is None:
            fn(*args)
        else:
            pl.when(when)(lambda: fn(*args))

    total[...] = jnp.zeros_like(total)

    def program_0():
        step("first", first)
        step("x0_send", x0_send, 1, "f", 0)
        step("z_send", z_send, 1, "f", 0)
        step("y_own0", y_send, 0, 1, 0)
        step("pair0", pair_send, 0)
        step("own_sib", lambda: links.send(("S",), amp(0, 0, 0), sibling))
        step("own_sib_in", lambda: links.recv(("O",), amp(0, 0, 1), sibling))
        step("x0_send", x0_send, -1, "b", 1)
        step("pair1", pair_send, 1)
        step("z_send", z_send, -1, "b", 1)
        step("x0_send", x0_send, 1, "f", 1)
        step("z_send", z_send, 1, "f", 1)
        step("x0_send", x0_send, -1, "b", 0)
        step("z_send", z_send, -1, "b", 0)
        step("y_own1", y_send, 0, 1, 1)
        step("y01a", y_on, 0, 1, 0)
        step("x0", x0_first)
        step("y01b", y_on, 0, 1, 1)
        step("x0r", x0_rest)
        step("pair0", pair_on, 0)
        step("z_first", z_first)
        step("y02a", y_on, 0, 2, 0)
        step("pair1", pair_on, 1)
        step("y02b", y_on, 0, 2, 1)
        step("xf0", x_far, 0)
        step("z_rest", z_rest)
        step("y11a", y_on, 1, 1, 0)
        step("x1", x1_first)
        step("y03a", y_on, 0, 3, 0)
        step("load", loads[1].wait)
        step("h0", take_holes, (0, 0), (0, -1), (0, 1), (0, 2))
        step("y11b", y_on, 1, 1, 1)
        step("y03b", y_on, 0, 3, 1)
        step("z_far", z_far)
        step("y12a", y_on, 1, 2, 0)
        step("x1r", x1_rest)
        step("h1", take_holes, (-1, 0), (1, 0), (2, 0))
        step("y12b", y_on, 1, 2, 1)
        step("y04", y_on, 0, 4, 0)
        step("y04", y_on, 0, 4, 1)
        step("h2", take_holes, (-1, -1), (-1, 1), (1, -1), (1, 1))
        step("y13a", y_on, 1, 3, 0)
        step("x2", x2_all)
        step("y13b", y_on, 1, 3, 1)
        step("h2", take_holes, (2, -1), (2, 1))
        step("xf-1", x_far, -1)
        step("xf1", x_far, 1)
        step("h3", take_holes, (-1, 2), (1, 2))
        step("y14", y_on, 1, 4, 0)
        step("y14", y_on, 1, 4, 1)
        step("p0", get_particles, (0, 0), (-1, 0), (1, 0), (0, -1))
        step("xf2", x_far, 2)
        step("p1", get_particles, (0, 1), (0, 2), (2, 0), (-1, -1))
        step("h3", take_holes, (2, 2))
        step("p2", get_particles, (-1, 1), (1, -1), (1, 1), (-1, 2))
        step("p3", get_particles, (1, 2), (2, -1), (2, 1), (2, 2))

    def program_1():
        step("first", first)
        step("own_sib", lambda: links.send(("O",), amp(0, 0, 1), sibling))
        step("own_sib_in", lambda: links.recv(("S",), amp(0, 0, 0), sibling))
        step("first_in", first_in)
        step("second", second_out)
        step("second_in", second_in)
        step("p_own", p_own)
        step("ps0", p_sibs, (0, 0))
        step("load", loads[1].wait)
        step("pa", pa_all)
        step("pb0", pb_all, 0)
        step("ps1", p_sibs, (0, 1), (0, -1), (1, 0), (-1, 0))
        step("h0", get_holes, (0, 0), (0, -1), (0, 1))
        step("h1", get_holes, (0, 2), (-1, 0), (1, 0))
        step("h1", get_holes, (2, 0))
        step("pa_far", pa_far)
        step("pbb0", pb_far, 0)
        step("ps2", p_sibs, (0, 2), (2, 0))
        step("pb-1", pb_all, -1)
        step("pb1", pb_all, 1)
        step("ps3", p_sibs, (-1, -1), (-1, 1), (1, -1), (1, 1))
        step("h2", get_holes, (-1, -1), (-1, 1), (1, -1), (1, 1))
        step("pb2", pb_all, 2)
        step("pbb-1", pb_far, -1)
        step("pbb1", pb_far, 1)
        step("ps4", p_sibs, (-1, 2), (1, 2), (2, -1), (2, 1))
        step("h3", get_holes, (2, -1), (2, 1))
        step("pbb2", pb_far, 2)
        step("ps5", p_sibs, (2, 2))
        step("h3", get_holes, (-1, 2), (1, 2))
        step("rows", get_rows)
        step("p0", take_particles, (0, 0), (-1, 0), (1, 0), (0, -1), (0, 1), (0, 2), (2, 0), (-1, -1))
        step("p1", take_particles, (-1, 1), (1, -1), (1, 1), (-1, 2), (1, 2), (2, -1), (2, 1), (2, 2))
        step("h3", get_holes, (2, 2))

    def drain_0():
        links.drain("T", col.at[pl.ds(0, 30)], sibling)
        links.drain("S", col.at[pl.ds(0, 31)], sibling)
        links.drain("y", row.at[pl.ds(0, 30)], sibling)
        links.drain("R", row.at[pl.ds(0, 15)], sibling)

    def drain_1():
        links.drain("O", col.at[pl.ds(0, 1)], sibling)
        links.drain("p", slab.at[pl.ds(0, 30)], sibling)
        links.drain("q", slab, sibling)
        pl.when(second_moves)(lambda: links.copy(("2",), moved, moved, sibling).wait_send())

    pl.when(lead)(program_0)
    pl.when(other)(program_1)

    def finish():
        for load in loads[2:5]:
            load.wait()
        occ_col = jnp.transpose(jnp.broadcast_to(occ_ref[...], (TILE, ROWS)))
        for i in range(2):
            for j in range(2):
                rows, cols = pl.ds(i * TILE, TILE), pl.ds(j * TILE, TILE)
                keep = screen[i : i + 1, j : j + 1].astype(jnp.float32)
                a = amps[rows, cols].astype(jnp.float32)
                denom = virt_ref[:, cols] - occ_col[i * TILE : (i + 1) * TILE]
                ladders = total[rows, cols]
                res = keep * (direct[rows, cols].astype(jnp.float32) + ladders - denom * a)
                step_ref[rows, cols] = res / denom

    step("finish", finish)
    pl.when(lead)(drain_0)
    pl.when(other)(drain_1)
    pl.when(lead | first_moves)(lambda: links.copy(("1", 0), moved.at[0], moved.at[0], sibling).wait_send())
    assert max(map(len, links.ids)) <= N_COPIES


def on_device(amplitudes, screen, hole_ints, particle_ints, direct_ints, occ_energy, virt_energy):
    vmem, hbm = pl.BlockSpec(memory_space=pltpu.VMEM), pl.BlockSpec(memory_space=pltpu.HBM)
    change = pl.pallas_call(
        kernel,
        out_shape=jax.ShapeDtypeStruct((ROWS, COLS), jnp.float32),
        in_specs=[hbm] * 7,
        out_specs=vmem,
        scratch_shapes=[
            pltpu.VMEM((ROWS, COLS), jnp.bfloat16),
            pltpu.VMEM((ROWS, COLS), jnp.bfloat16),
            pltpu.VMEM((ROWS, 8192), jnp.bfloat16),
            pltpu.VMEM((32, ROWS, COLS), jnp.bfloat16),
            pltpu.VMEM((32, ROWS, COLS), jnp.bfloat16),
            pltpu.VMEM((32, ROWS, TILE), jnp.bfloat16),
            pltpu.VMEM((2, ROWS, TILE), jnp.bfloat16),
            pltpu.VMEM((ROWS, COLS), jnp.float32),
            pltpu.VMEM((1, ROWS), jnp.float32),
            pltpu.VMEM((1, COLS), jnp.float32),
            pltpu.VMEM((2, 2), jnp.int32),
            pltpu.SemaphoreType.DMA((9,)),
            pltpu.SemaphoreType.DMA((N_COPIES,)),
            pltpu.SemaphoreType.DMA((8,)),
        ],
        compiler_params=pltpu.CompilerParams(
            collective_id=0, has_side_effects=True, vmem_limit_bytes=62 * 2**20
        ),
        name="ladders",
    )(
        screen,
        amplitudes,
        hole_ints,
        particle_ints,
        direct_ints,
        occ_energy.reshape(1, ROWS),
        virt_energy.reshape(1, COLS),
    )
    denom = virt_energy[None, :] - occ_energy[:, None]
    return change * denom, (amplitudes.astype(jnp.float32) + change).astype(jnp.bfloat16)


def solution(mesh):
    in_specs = (
        P("occ", "virt"),
        P("occ", "virt"),
        P("occ", None),
        P("virt", "occ"),
        P("occ", "virt"),
        P("occ"),
        P("virt"),
    )
    out_specs = (P("occ", "virt"), P("occ", "virt"))
    return jax.shard_map(
        on_device, mesh=mesh, in_specs=in_specs, out_specs=out_specs, check_vma=False
    )
```

```python
import math

import jax
import jax.numpy as jnp
from jax import lax
from jax.experimental import pallas as pl
from jax.experimental.pallas import tpu as pltpu
from jax.sharding import PartitionSpec as P

MESH = pl.DeviceIdType.MESH
NX, NZH, NY, NZL = 4, 4, 8, 2
ROWS, COLS, HALF, TILE = 256, 256, 128, 128


def wrap(a, n):
    return lax.rem(a + n, n)


class Links:
    KINDS = "TOqySRp12"
    ON_CORE_0 = "TOqy"

    def __init__(self, send_sem, recv_sem):
        self.send_sem, self.recv_sem = send_sem, recv_sem
        self.ids, self.sent = ({}, {}), {}

    def copy(self, name, src, dst, device):
        ids = self.ids[name[0][0] not in self.ON_CORE_0]
        n = ids.setdefault(name, len(ids))
        return pltpu.make_async_remote_copy(
            src_ref=src,
            dst_ref=dst,
            send_sem=self.send_sem.at[self.KINDS.index(name[0][0])],
            recv_sem=self.recv_sem.at[n],
            device_id=device,
            device_id_type=MESH,
        )

    def send(self, name, src, device, dst=None):
        self.copy(name, src, src if dst is None else dst, device).start()
        self.sent[name] = math.prod(src.shape)

    def recv(self, name, dst, device):
        self.copy(name, dst, dst, device).wait_recv()

    def drain(self, kind, everything, device):
        sent = sum(size for name, size in self.sent.items() if name[0][0] == kind)
        assert sent == math.prod(everything.shape)
        name = next(name for name in self.sent if name[0][0] == kind)
        self.copy(name, everything, everything, device).wait_send()


N_COPIES = 80


def kernel(
    screen_hbm,
    amps_hbm,
    hole_hbm,
    part_hbm,
    direct_hbm,
    occ_hbm,
    virt_hbm,
    step_ref,
    amps,
    direct,
    hole_ints,
    col,
    row,
    slab,
    moved,
    total,
    occ_ref,
    virt_ref,
    screen,
    part,
    send_sem,
    recv_sem,
    load_sem,
):
    o, v = lax.axis_index("occ"), lax.axis_index("virt")
    core, chip = lax.rem(o, 2), o // 2
    x, zh = lax.rem(chip, NX), chip // NX
    zl, y = v // NY, lax.rem(v, NY)
    yl, y2 = lax.rem(y, 4), y // 4

    def occ_of(zh, x, core):
        return (zh * NX + x) * 2 + core

    def zx(dz, dx):
        return wrap(zh + dz, NZH), wrap(x + dx, NX)

    def at_zx(dz, dx):
        return (occ_of(*zx(dz, dx), core), v)

    def at_y(dy):
        return (o, zl * NY + wrap(y + dy, NY))

    def flipped(zh, hi, lo):
        return lax.rem(zh // 2 + hi, 2) * 2 + lax.rem(zh + lo, 2)

    sibling = (occ_of(zh, x, 1 - core), v)
    partner = (o, (1 - zl) * NY + y)
    zh_1 = flipped(zh, zl, y2)
    first_to = (occ_of(zh_1, wrap(x + yl, NX), 1), v)
    first_from = [(occ_of(zh_1, wrap(x - yl, NX), c), v) for c in range(2)]
    first_moves = v != 0
    v_2 = lax.rem(zh // 2 + zl, 2) * NY + lax.rem(zh + y2, 2) * 4 + wrap(x - yl, 4)
    second = (o, v_2)
    second_moves = v_2 != v
    lead, other = core == 0, core == 1

    def signal(sem, device):
        pl.semaphore_signal(sem, inc=1, device_id=device, device_id_type=MESH)

    def count(*flags):
        return sum(flag.astype(jnp.int32) for flag in flags)

    loads = [
        pltpu.make_async_copy(src, dst, load_sem.at[n])
        for n, (src, dst) in enumerate(
            (
                (amps_hbm, amps),
                (hole_hbm, hole_ints),
                (direct_hbm, direct),
                (occ_hbm, occ_ref),
                (virt_hbm, virt_ref),
                (screen_hbm, screen),
                (part_hbm, part),
            )
        )
    ]
    loads[0].start()
    loads[5].start()
    loads[6].start()

    barrier = pltpu.get_barrier_semaphore()
    for device in first_from:
        pl.when(other & first_moves)(lambda device=device: signal(barrier, device))
    pl.when(other & second_moves)(lambda: signal(barrier, second))
    for device in (at_zx(1, 0), at_zx(-1, 0), at_zx(0, 1), at_zx(0, -1), sibling):
        signal(barrier, device)
    for device in (at_y(1), at_y(-1), partner):
        pl.when(lead)(lambda device=device: signal(barrier, device))

    for load in loads[1:5]:
        load.start()
    loads[0].wait()
    loads[6].wait()
    loads[5].wait()
    for i in range(2):
        for j in range(2):
            rows, cols = pl.ds(i * TILE, TILE), pl.ds(j * TILE, TILE)
            keep = screen[i : i + 1, j : j + 1].astype(jnp.float32)
            tile = (amps[rows, cols].astype(jnp.float32) * keep).astype(jnp.bfloat16)
            col[o, rows, cols] = tile
            row[v * 2 + core, rows, cols] = tile

    pl.semaphore_wait(barrier, 5 + 3 * count(lead) + count(first_moves, other & second_moves))

    links = Links(send_sem, recv_sem)

    WAYS = ((1, "f", 0), (-1, "b", 1))

    def amp(dz, dx, h=None):
        zz, xx = zx(dz, dx)
        c = (zz * NX + xx) * 2
        return col.at[pl.ds(c, 2)] if h is None else col.at[c + h]


    def to_sib(dz, dx):
        links.send(("S", dz, dx), amp(dz, dx), sibling)

    def z_send(way, tag, h):
        links.send(("Tz", tag, h), amp(0, 0, h), at_zx(way, 0))

    def x_send(dz, h):
        for way, tag, _ in WAYS:
            links.send(("Tx", dz, tag, h), amp(dz, 0, h), at_zx(0, way))

    def x0_send(way, tag, h):
        links.send(("Tx", 0, tag, h), amp(0, 0, h), at_zx(0, way))

    def x_recv(dz, way, tag, h):
        links.recv(("Tx", dz, tag, h), amp(dz, -way, h), at_zx(0, -way))

    def x_pass(dz, way, tag, h):
        links.send(("Txx", dz, tag), amp(dz, -way, h), at_zx(0, way))

    def z_first():
        for way, tag, h in WAYS:
            links.recv(("Tz", tag, h), amp(-way, 0, h), at_zx(-way, 0))
            links.send(("Tzz", tag), amp(-way, 0, h), at_zx(way, 0))
            x_send(-way, h)

    def z_rest():
        for way, tag, h in WAYS:
            links.recv(("Tz", tag, 1 - h), amp(-way, 0, 1 - h), at_zx(-way, 0))
            x_send(-way, 1 - h)
        for way, _, _ in WAYS:
            to_sib(-way, 0)

    def z_far():
        for way, tag, h in WAYS:
            links.recv(("Tzz", tag), amp(2, 0, h), at_zx(-way, 0))
        for way, tag, h in WAYS:
            links.send(("Tx", 2, tag), amp(2, 0), at_zx(0, way))
        to_sib(2, 0)

    def x0_first():
        for way, tag, h in WAYS:
            x_recv(0, way, tag, h)
            x_pass(0, way, tag, h)

    def x0_rest():
        for way, tag, h in WAYS:
            x_recv(0, way, tag, 1 - h)
            to_sib(0, -way)

    def x1_first():
        for dz, early in ((-1, 0), (1, 1)):
            for way, tag, h in WAYS:
                x_recv(dz, way, tag, early)
                if h == early:
                    x_pass(dz, way, tag, h)

    def x1_rest():
        for dz, early in ((-1, 0), (1, 1)):
            for way, tag, h in WAYS:
                x_recv(dz, way, tag, 1 - early)
                if h != early:
                    x_pass(dz, way, tag, h)
            for way, _, _ in WAYS:
                to_sib(dz, -way)

    def x2_all():
        for way, tag, h in WAYS:
            links.recv(("Tx", 2, tag), amp(2, -way), at_zx(0, -way))
            x_pass(2, way, tag, h)
            to_sib(2, -way)

    def x_far(dz):
        for way, tag, h in WAYS:
            links.recv(("Txx", dz, tag), amp(dz, 2, h), at_zx(0, -way))
        to_sib(dz, 2)


    def turned(a, b, h):
        return (a, b) if h == 0 else (b, a)

    def ints(dz, dx, h=None, part=None):
        zz, xx = zx(dz, dx)
        p = (zz * NX + xx) * 2
        ref = slab.at[pl.ds(p, 2)] if h is None else slab.at[p + h]
        return ref if part is None else ref.at[pl.ds(part * HALF, HALF)]

    def p_send(a):
        for half in range(2):
            for way, tag, _ in WAYS:
                links.send(("pb", a, half, tag), ints(*turned(a, 0, half), half), at_zx(*turned(0, way, half)))

    def p_own():
        for half in range(2):
            for way, tag, _ in WAYS:
                links.send(("pa", half, tag), ints(0, 0, half), at_zx(*turned(way, 0, half)))
        p_send(0)

    def pa_all():
        for half in range(2):
            for way, tag, h in WAYS:
                here = turned(-way, 0, half)
                links.recv(("pa", half, tag), ints(*here, half), at_zx(*here))
                links.send(("paa", half, tag), ints(*here, half, h), at_zx(*turned(way, 0, half)))
        for way, _, _ in WAYS:
            p_send(-way)

    def pa_far():
        for half in range(2):
            for way, tag, h in WAYS:
                links.recv(
                    ("paa", half, tag), ints(*turned(2, 0, half), half, h), at_zx(*turned(-way, 0, half))
                )
        p_send(2)

    def pb_all(a):
        for half in range(2):
            for way, tag, h in WAYS:
                here = turned(a, -way, half)
                links.recv(("pb", a, half, tag), ints(*here, half), at_zx(*turned(0, -way, half)))
                links.send(("pbb", a, half, tag), ints(*here, half, h), at_zx(*turned(0, way, half)))

    def pb_far(a):
        for half in range(2):
            for way, tag, h in WAYS:
                links.recv(
                    ("pbb", a, half, tag),
                    ints(*turned(a, 2, half), half, h),
                    at_zx(*turned(0, -way, half)),
                )

    def p_sibs(*places):
        for place in places:
            links.send(("q",) + place, ints(*place), sibling)

    def strip(e, dy, h=None):
        k = ((zl if e == 0 else 1 - zl) * NY + wrap(y + dy, NY)) * 2
        return row.at[pl.ds(k, 2)] if h is None else row.at[k + h]

    def y_send(e, hop, half):
        for way, tag, h in WAYS:
            if hop < 4 or h == half:
                dst = strip(e, -way * (hop - 1), half)
                src = amp(0, 0, half) if (e, hop) == (0, 1) else dst
                links.send(("y", e, hop, tag, half), src, at_y(way), dst)

    def y_on(e, hop, half):
        for way, tag, h in WAYS:
            if hop < 4 or h == half:
                links.recv(("y", e, hop, tag, half), strip(e, -way * hop, half), at_y(-way))
        if hop < 4:
            y_send(e, hop + 1, half)
        if half == 1:
            for dy in (hop, -hop) if hop < 4 else (4,):
                row_sib(e, dy)

    def row_sib(e, dy):
        links.send(("R", e, dy), strip(e, dy, 1), sibling)

    def pair_send(half):
        links.send(("ypair", half), amp(0, 0, half), partner, strip(0, 0, half))

    def pair_on(half):
        links.recv(("ypair", half), strip(1, 0, half), partner)
        y_send(1, 1, half)
        if half == 1:
            row_sib(1, 0)


    def add_hole(dz, dx, block):
        zz, xx = zx(dz, dx)
        ints_ = hole_ints[:, pl.ds(pl.multiple_of((zz * NX + xx) * 512, 512), 512)]
        total[...] += jnp.dot(
            ints_, block[...].reshape(2 * ROWS, COLS), preferred_element_type=jnp.float32
        )

    def take_holes(*places):
        for place in places:
            add_hole(*place, amp(*place))

    def get_holes(*places):
        for place in places:
            if place != (0, 0):
                links.recv(("S",) + place, amp(*place), sibling)
            add_hole(*place, amp(*place))

    def add_particles(places):
        rows, blocks = [], []
        for dz, dx in places:
            zz, xx = zx(dz, dx)
            p = (zz * NX + xx) * 2
            k = lax.rem(zz // 2 + zl, 2) * NY + lax.rem(zz + y2, 2) * 4 + wrap(xx - yl, 4)
            rows.append(row[k * 2 + core])
            blocks.append(jnp.concatenate([slab[p], slab[p + 1]], axis=1))
        total[...] += jnp.dot(
            jnp.concatenate(rows, axis=1),
            jnp.concatenate(blocks, axis=0),
            preferred_element_type=jnp.float32,
        )

    def take_particles(*places):
        for n in range(0, len(places), 4):
            add_particles(places[n : n + 4])

    def get_rows():
        for e in range(2):
            for dy in range(e == 0, NY):
                links.recv(("R", e, dy if dy <= 4 else dy - NY), strip(e, dy, 1), sibling)

    def get_particles(*places):
        for place in places:
            links.recv(("q",) + place, ints(*place), sibling)
        take_particles(*places)


    def first():
        pl.when(lead)(lambda: links.send(("1", 0), part, first_to, moved.at[0]))
        pl.when(other & first_moves)(lambda: links.send(("1", 1), part, first_to, moved.at[1]))
        pl.when(other & jnp.logical_not(first_moves))(
            lambda: pltpu.make_async_copy(part, moved.at[1], load_sem.at[7]).start()
        )

    def first_in():
        links.recv(("1", 0), moved.at[0], first_from[0])
        pl.when(first_moves)(lambda: links.recv(("1", 1), moved.at[1], first_from[1]))
        pl.when(jnp.logical_not(first_moves))(
            lambda: pltpu.make_async_copy(part, moved.at[1], load_sem.at[7]).wait()
        )

    def second_out():
        pl.when(second_moves)(lambda: links.send(("2",), moved, second, ints(0, 0)))
        pl.when(jnp.logical_not(second_moves))(
            lambda: pltpu.make_async_copy(moved, ints(0, 0), load_sem.at[8]).start()
        )

    def second_in():
        pl.when(second_moves)(lambda: links.recv(("2",), ints(0, 0), second))
        pl.when(jnp.logical_not(second_moves))(
            lambda: pltpu.make_async_copy(moved, ints(0, 0), load_sem.at[8]).wait()
        )

    def step(name, fn, *args, when=None):
        if when is None:
            fn(*args)
        else:
            pl.when(when)(lambda: fn(*args))

    total[...] = jnp.zeros_like(total)

    def program_0():
        step("first", first)
        step("x0_send", x0_send, 1, "f", 0)
        step("z_send", z_send, 1, "f", 0)
        step("y_own0", y_send, 0, 1, 0)
        step("pair0", pair_send, 0)
        step("own_sib", lambda: links.send(("S",), amp(0, 0, 0), sibling))
        step("own_sib_in", lambda: links.recv(("O",), amp(0, 0, 1), sibling))
        step("x0_send", x0_send, -1, "b", 1)
        step("pair1", pair_send, 1)
        step("z_send", z_send, -1, "b", 1)
        step("x0_send", x0_send, 1, "f", 1)
        step("z_send", z_send, 1, "f", 1)
        step("x0_send", x0_send, -1, "b", 0)
        step("z_send", z_send, -1, "b", 0)
        step("y_own1", y_send, 0, 1, 1)
        step("y01a", y_on, 0, 1, 0)
        step("x0", x0_first)
        step("y01b", y_on, 0, 1, 1)
        step("x0r", x0_rest)
        step("pair0", pair_on, 0)
        step("z_first", z_first)
        step("y02a", y_on, 0, 2, 0)
        step("pair1", pair_on, 1)
        step("y02b", y_on, 0, 2, 1)
        step("xf0", x_far, 0)
        step("z_rest", z_rest)
        step("y11a", y_on, 1, 1, 0)
        step("x1", x1_first)
        step("y03a", y_on, 0, 3, 0)
        step("load", loads[1].wait)
        step("h0", take_holes, (0, 0), (0, -1), (0, 1), (0, 2))
        step("y11b", y_on, 1, 1, 1)
        step("y03b", y_on, 0, 3, 1)
        step("z_far", z_far)
        step("y12a", y_on, 1, 2, 0)
        step("x1r", x1_rest)
        step("h1", take_holes, (-1, 0), (1, 0), (2, 0))
        step("y12b", y_on, 1, 2, 1)
        step("y04", y_on, 0, 4, 0)
        step("y04", y_on, 0, 4, 1)
        step("h2", take_holes, (-1, -1), (-1, 1), (1, -1), (1, 1))
        step("y13a", y_on, 1, 3, 0)
        step("x2", x2_all)
        step("y13b", y_on, 1, 3, 1)
        step("h2", take_holes, (2, -1), (2, 1))
        step("xf-1", x_far, -1)
        step("xf1", x_far, 1)
        step("h3", take_holes, (-1, 2), (1, 2))
        step("y14", y_on, 1, 4, 0)
        step("y14", y_on, 1, 4, 1)
        step("p0", get_particles, (0, 0), (-1, 0), (1, 0), (0, -1))
        step("xf2", x_far, 2)
        step("p1", get_particles, (0, 1), (0, 2), (2, 0), (-1, -1))
        step("h3", take_holes, (2, 2))
        step("p2", get_particles, (-1, 1), (1, -1), (1, 1), (-1, 2))
        step("p3", get_particles, (1, 2), (2, -1), (2, 1), (2, 2))

    def program_1():
        step("first", first)
        step("own_sib", lambda: links.send(("O",), amp(0, 0, 1), sibling))
        step("own_sib_in", lambda: links.recv(("S",), amp(0, 0, 0), sibling))
        step("first_in", first_in)
        step("second", second_out)
        step("second_in", second_in)
        step("p_own", p_own)
        step("ps0", p_sibs, (0, 0))
        step("load", loads[1].wait)
        step("pa", pa_all)
        step("pb0", pb_all, 0)
        step("ps1", p_sibs, (0, 1), (0, -1), (1, 0), (-1, 0))
        step("h0", get_holes, (0, 0), (0, -1), (0, 1))
        step("h1", get_holes, (0, 2), (-1, 0), (1, 0))
        step("h1", get_holes, (2, 0))
        step("pa_far", pa_far)
        step("pbb0", pb_far, 0)
        step("ps2", p_sibs, (0, 2), (2, 0))
        step("pb-1", pb_all, -1)
        step("pb1", pb_all, 1)
        step("ps3", p_sibs, (-1, -1), (-1, 1), (1, -1), (1, 1))
        step("h2", get_holes, (-1, -1), (-1, 1), (1, -1), (1, 1))
        step("pb2", pb_all, 2)
        step("pbb-1", pb_far, -1)
        step("pbb1", pb_far, 1)
        step("ps4", p_sibs, (-1, 2), (1, 2), (2, -1), (2, 1))
        step("h3", get_holes, (2, -1), (2, 1))
        step("pbb2", pb_far, 2)
        step("ps5", p_sibs, (2, 2))
        step("h3", get_holes, (-1, 2), (1, 2))
        step("rows", get_rows)
        step("p0", take_particles, (0, 0), (-1, 0), (1, 0), (0, -1), (0, 1), (0, 2), (2, 0), (-1, -1))
        step("p1", take_particles, (-1, 1), (1, -1), (1, 1), (-1, 2), (1, 2), (2, -1), (2, 1), (2, 2))
        step("h3", get_holes, (2, 2))

    def drain_0():
        links.drain("T", col.at[pl.ds(0, 30)], sibling)
        links.drain("S", col.at[pl.ds(0, 31)], sibling)
        links.drain("y", row.at[pl.ds(0, 30)], sibling)
        links.drain("R", row.at[pl.ds(0, 15)], sibling)

    def drain_1():
        links.drain("O", col.at[pl.ds(0, 1)], sibling)
        links.drain("p", slab.at[pl.ds(0, 30)], sibling)
        links.drain("q", slab, sibling)
        pl.when(second_moves)(lambda: links.copy(("2",), moved, moved, sibling).wait_send())

    pl.when(lead)(program_0)
    pl.when(other)(program_1)

    def finish():
        for load in loads[2:5]:
            load.wait()
        occ_col = jnp.transpose(jnp.broadcast_to(occ_ref[...], (TILE, ROWS)))
        for i in range(2):
            for j in range(2):
                rows, cols = pl.ds(i * TILE, TILE), pl.ds(j * TILE, TILE)
                keep = screen[i : i + 1, j : j + 1].astype(jnp.float32)
                a = amps[rows, cols].astype(jnp.float32)
                denom = virt_ref[:, cols] - occ_col[i * TILE : (i + 1) * TILE]
                ladders = total[rows, cols]
                res = keep * (direct[rows, cols].astype(jnp.float32) + ladders - denom * a)
                step_ref[rows, cols] = res / denom

    step("finish", finish)
    pl.when(lead)(drain_0)
    pl.when(other)(drain_1)
    pl.when(lead | first_moves)(lambda: links.copy(("1", 0), moved.at[0], moved.at[0], sibling).wait_send())
    assert max(map(len, links.ids)) <= N_COPIES


def on_device(amplitudes, screen, hole_ints, particle_ints, direct_ints, occ_energy, virt_energy):
    vmem, hbm = pl.BlockSpec(memory_space=pltpu.VMEM), pl.BlockSpec(memory_space=pltpu.HBM)
    change = pl.pallas_call(
        kernel,
        out_shape=jax.ShapeDtypeStruct((ROWS, COLS), jnp.float32),
        in_specs=[hbm] * 7,
        out_specs=vmem,
        scratch_shapes=[
            pltpu.VMEM((ROWS, COLS), jnp.bfloat16),
            pltpu.VMEM((ROWS, COLS), jnp.bfloat16),
            pltpu.VMEM((ROWS, 8192), jnp.bfloat16),
            pltpu.VMEM((32, ROWS, COLS), jnp.bfloat16),
            pltpu.VMEM((32, ROWS, COLS), jnp.bfloat16),
            pltpu.VMEM((32, ROWS, TILE), jnp.bfloat16),
            pltpu.VMEM((2, ROWS, TILE), jnp.bfloat16),
            pltpu.VMEM((ROWS, COLS), jnp.float32),
            pltpu.VMEM((1, ROWS), jnp.float32),
            pltpu.VMEM((1, COLS), jnp.float32),
            pltpu.VMEM((2, 2), jnp.int32),
            pltpu.VMEM((ROWS, TILE), jnp.bfloat16),
            pltpu.SemaphoreType.DMA((9,)),
            pltpu.SemaphoreType.DMA((N_COPIES,)),
            pltpu.SemaphoreType.DMA((9,)),
        ],
        compiler_params=pltpu.CompilerParams(
            collective_id=0, has_side_effects=True, vmem_limit_bytes=62 * 2**20
        ),
        name="ladders",
    )(
        screen,
        amplitudes,
        hole_ints,
        particle_ints,
        direct_ints,
        occ_energy.reshape(1, ROWS),
        virt_energy.reshape(1, COLS),
    )
    denom = virt_energy[None, :] - occ_energy[:, None]
    return change * denom, (amplitudes.astype(jnp.float32) + change).astype(jnp.bfloat16)


def solution(mesh):
    in_specs = (
        P("occ", "virt"),
        P("occ", "virt"),
        P("occ", None),
        P("virt", "occ"),
        P("occ", "virt"),
        P("occ"),
        P("virt"),
    )
    out_specs = (P("occ", "virt"), P("occ", "virt"))
    return jax.shard_map(
        on_device, mesh=mesh, in_specs=in_specs, out_specs=out_specs, check_vma=False
    )
```
